512 devices in a mesh: dp: 16 (over y, core), expert: 32 (over x, z).
Axes of the slice: x: 4, y: 8, z: 8, core: 2. Of those that a mesh axis runs over, the one named last changes fastest.
Arguments:
- tokens: bfloat16 [65536, 2048], P(('dp', 'expert')), may hold values from -6 to 6
- cotangent: bfloat16 [65536, 2048], P(('dp', 'expert')), may hold values from -5 to 5
- routes: int32 [65536, 1], P(('dp', 'expert')), may hold values from 0 to 7; in each aligned block of 128 rows (0 to 127, 128 to 255, ...) at most 18 rows name the same one
- expert_gates: float32 [65536, 1], P(('dp', 'expert')), may hold values from 0.1 to 1
- gate_proj: bfloat16 [2048, 6144], P(None, 'expert'), may hold values from -0.125 to 0.125
- up_proj: bfloat16 [2048, 6144], P(None, 'expert'), may hold values from -0.125 to 0.125
- down_proj: bfloat16 [6144, 2048], P('expert'), may hold values from -0.21875 to 0.21875
Outputs:
- grad_input: bfloat16 [65536, 2048], P(('dp', 'expert'))
- grad_gate: float32 [2048, 6144], P('dp', 'expert')
- grad_up: float32 [2048, 6144], P('dp', 'expert')
- grad_down: float32 [6144, 2048], P('expert', 'dp')
The draws below stay inside these ranges and needn't reach their ends.
Inputs may be any that keep to these rules, and one draw needn't show every extreme that they name: `routes`: each row names exactly one expert. Among the rows of one device no expert is named more than 18 times.
All inputs are finite; a program needn't handle non-finite values.
Results may differ from the reference program's by a relative error of at most 0.022.
Values may be sent and summed in bfloat16 or wider, within the bound.
A program may use at most 64 MiB of HBM per device.

```python
import math
import jax
import jax.numpy as jnp
import numpy as np
from jax import lax

D = 2048
HID = 768
EXPERTS = 8
TOP = 1
TOK_DEV = 128
MOST = 18
TOKENS = 65536
N_DP = 16
N_EXPERT = 32


def strengthened(result, key, source, target, blocks, factor):
    owner, partner = [(jnp.arange(result.shape[position]) // (result.shape[position] // blocks)).reshape([-1 if axis == position else 1 for axis in range(result.ndim)]) for position in (source, target)]
    chosen = jax.random.permutation(key, blocks)[partner]
    strong = (owner == chosen) | (owner == (partner + blocks // 2) % blocks)
    return jnp.where(strong, factor * result, result)


def steps_of(rng, extent, split, smallest, largest):
    loudness, own = 1.0, jax.random.fold_in(rng, 6)
    for axis_at, shards_of in split:
        draws = jnp.exp(jax.random.uniform(jax.random.fold_in(own, axis_at), (shards_of,), jnp.float32, smallest / len(split), largest / len(split)))
        loudness = loudness * jnp.repeat(draws, extent[axis_at] // shards_of).reshape([-1 if axis == axis_at else 1 for axis in range(len(extent))])
    return loudness


def deal_out(stream_key, own, number, rows, number_of, top, most, lean):
    order = jax.random.permutation(stream_key, number_of)
    crowded, usual = shares(number_of, rows * top, most, lean, True), shares(number_of, rows * top, most, lean, False)
    places = jnp.arange(number_of)

    def named(lengths, offset_by):
        used = int((lengths > 0).sum())
        fixed = max(1, used // 4)
        moved = fixed + (places - fixed + offset_by * (used - fixed)) % max(1, number_of - fixed)
        return jnp.zeros((number_of,), jnp.int32).at[order[jnp.where(places < fixed, places, moved)]].set(jnp.asarray(lengths, jnp.int32))

    lengths = jnp.where(number % 4 == 0, named(crowded, number // 4), named(usual, number - number // 4 - 1))
    mixed = jax.random.permutation(jax.random.fold_in(own, 3), number_of)
    giver, taker = mixed[0:number_of // 2 * 2:2], mixed[1:number_of // 2 * 2:2]
    slack = jnp.minimum(lengths[giver] - 1, most - lengths[taker]) // 2
    slack = jnp.where((giver == order[0]) | (taker == order[0]) | (lengths[taker] == 0), 0, jnp.maximum(slack, 0))
    moved = jax.random.randint(jax.random.fold_in(own, 4), (number_of // 2,), 0, 1 << 20) % (slack + 1)
    lengths = lengths.at[giver].add(-moved).at[taker].add(moved)
    labels = jnp.searchsorted(jnp.cumsum(lengths), jnp.arange(rows * top), side="right").astype(jnp.int32)
    grid = labels.reshape(top, rows).T
    grid = grid[jax.random.permutation(jax.random.fold_in(own, 1), rows)]
    offset_by = jax.random.randint(jax.random.fold_in(own, 2), (rows, 1), 0, top)
    return jnp.take_along_axis(grid, (jnp.arange(top)[None, :] + offset_by) % top, axis=1)


def shares(number_of, total, reach, lean, full):
    weights = [(1 << 20) // math.isqrt(standing ** lean) + 1 for standing in range(1, number_of + 1)]
    largest = reach if full else min(reach, max(-(-total // number_of), total * weights[0] // sum(weights)))
    least = 1 if total - largest >= number_of - 1 else 0
    counts, rest = [largest] + [least] * (number_of - 1), total - largest - least * (number_of - 1)
    while rest > 0:
        movable = [i for i in range(1, number_of) if counts[i] < largest] or [i for i in range(1, number_of) if counts[i] < reach]
        pool, budget = sum([weights[i] for i in movable]), rest
        for i in movable:
            extra = min(reach - counts[i], max(1, budget * weights[i] // pool), rest)
            counts[i] = counts[i] + extra
            rest = rest - extra
    return np.array(counts)


def noise(stream_key, dims, deviation, bound, shards=(), held_as=jnp.bfloat16):
    drawn = jax.random.normal(stream_key, dims, jnp.float32) * deviation
    if len(shards) > 0:
        drawn = steps_of(stream_key, dims, shards, -0.22, 0.18) * drawn
    return jnp.clip(drawn, min=-bound, max=bound).astype(held_as)


def bell_draw_with(stream_key, shape, deviation, most, pieces, heavy, kind=jnp.bfloat16):
    result = deviation * jax.random.normal(stream_key, shape, jnp.float32)
    if pieces:
        result = result * steps_of(stream_key, shape, pieces, -0.22, 0.18)
    return jnp.clip(strengthened(result, jax.random.fold_in(stream_key, 3), *heavy), -most, most).astype(kind)


def setup_inputs(seed: int = 0) -> dict:
    keys = jax.random.split(jax.random.key(seed), 8)
    tokens = noise(keys[0], (TOKENS, D), 1.0, 6.0, ((0, 512),))
    cotangent = bell_draw_with(keys[1], (TOKENS, D), 0.2, 5.0, ((0, 512),), (0, 1, 512, 6.0))
    routes_keys = jax.random.split(jax.random.fold_in(keys[2], 1), TOKENS // TOK_DEV)
    routes_turns = jax.random.permutation(jax.random.fold_in(keys[2], 3), TOKENS // TOK_DEV)
    routes = jax.vmap(lambda own, number: deal_out(jax.random.fold_in(keys[2], 2), own, number, TOK_DEV, EXPERTS, TOP, MOST, 0))(routes_keys, routes_turns).reshape((TOKENS, TOP))
    expert_gates = jnp.clip(0.1 + 0.9 * jax.random.uniform(keys[3], (TOKENS, TOP), jnp.float32) ** steps_of(keys[3], (TOKENS, TOP), ((0, 512),), -0.2, 0.2), 0.1, 1.0)
    gate_proj = noise(keys[4], (D, EXPERTS * HID), D ** -0.5, 0.125, ((1, 32),))
    up_proj = noise(keys[5], (D, EXPERTS * HID), D ** -0.5, 0.125, ((1, 32),))
    down_proj = noise(keys[6], (EXPERTS * HID, D), HID ** -0.5, 0.21875, ((0, 32),))
    return {"tokens": tokens, "cotangent": cotangent, "routes": routes, "expert_gates": expert_gates, "gate_proj": gate_proj, "up_proj": up_proj, "down_proj": down_proj}


def slice_terms(group_x, scaled, gate_cols, up_cols, down_rows):
    pre_gate = jnp.dot(group_x, gate_cols, preferred_element_type=jnp.float32)
    pre_up = jnp.dot(group_x, up_cols, preferred_element_type=jnp.float32)
    gate_sig = jax.nn.sigmoid(pre_gate)
    hidden = (pre_gate * gate_sig * pre_up).astype(jnp.bfloat16)
    d_hidden = jnp.dot(scaled, down_rows.T, preferred_element_type=jnp.float32)
    d_gate = (d_hidden * pre_up * gate_sig * (1.0 + pre_gate * (1.0 - gate_sig))).astype(jnp.bfloat16)
    d_up = (d_hidden * pre_gate * gate_sig).astype(jnp.bfloat16)
    slice_input = (jnp.dot(d_gate, gate_cols.T, preferred_element_type=jnp.float32)
                   + jnp.dot(d_up, up_cols.T, preferred_element_type=jnp.float32)).astype(jnp.bfloat16)
    part_down = jnp.dot(hidden.T, scaled, preferred_element_type=jnp.float32)
    part_gate = jnp.dot(group_x.T, d_gate, preferred_element_type=jnp.float32)
    part_up = jnp.dot(group_x.T, d_up, preferred_element_type=jnp.float32)
    return slice_input, part_gate, part_up, part_down


def rounded(value):
    return lax.optimization_barrier(value.astype(jnp.bfloat16)).astype(jnp.float32)


def reference(tokens, cotangent, routes, expert_gates, gate_proj, up_proj, down_proj):
    group_size = N_EXPERT // EXPERTS
    hid_dev = HID // group_size
    group_rows = TOK_DEV * N_EXPERT
    capacity = N_EXPERT * MOST
    assigned = group_rows * TOP

    def one_group(totals, group_id):
        start = group_id * group_rows
        group_tok = lax.dynamic_slice_in_dim(tokens, start, group_rows, 0)
        group_dy = lax.dynamic_slice_in_dim(cotangent, start, group_rows, 0)
        flat_routes = lax.dynamic_slice_in_dim(routes, start, group_rows, 0).reshape(-1)
        weights = lax.dynamic_slice_in_dim(expert_gates, start, group_rows, 0).reshape(-1)
        grad_rows = jnp.zeros((group_rows, D), jnp.float32)
        list_gate, list_up, list_down = [], [], []
        for expert_id in range(EXPERTS):
            picked = jnp.nonzero(flat_routes == expert_id, size=capacity, fill_value=assigned)[0].astype(jnp.int32)
            owners = (picked // TOP).astype(jnp.int32)
            group_x = jnp.take(group_tok, owners, axis=0, mode="fill", fill_value=0)
            gate_vals = jnp.take(weights, picked, mode="fill", fill_value=0)
            scaled = (jnp.take(group_dy, owners, axis=0, mode="fill", fill_value=0).astype(jnp.float32)
                      * gate_vals[:, None]).astype(jnp.bfloat16)
            for piece_id in range(group_size):
                first = expert_id * HID + piece_id * hid_dev
                slice_input, part_gate, part_up, part_down = slice_terms(
                    group_x, scaled, gate_proj[:, first:first + hid_dev],
                    up_proj[:, first:first + hid_dev], down_proj[first:first + hid_dev, :])
                grad_rows = grad_rows.at[owners].add(slice_input.astype(jnp.float32), mode="drop")
                list_gate.append(part_gate)
                list_up.append(part_up)
                list_down.append(part_down)
        total_gate = totals[0] + rounded(jnp.concatenate(list_gate, 1))
        total_up = totals[1] + rounded(jnp.concatenate(list_up, 1))
        total_down = totals[2] + rounded(jnp.concatenate(list_down, 0))
        return (total_gate, total_up, total_down), grad_rows.astype(jnp.bfloat16)

    initial = (jnp.zeros((D, EXPERTS * HID), jnp.float32), jnp.zeros((D, EXPERTS * HID), jnp.float32),
               jnp.zeros((EXPERTS * HID, D), jnp.float32))
    sums, grad_input = lax.scan(one_group, initial, jnp.arange(N_DP, dtype=jnp.int32))
    return grad_input.reshape(TOKENS, D), sums[0], sums[1], sums[2]
```

```python
import jax
import jax.numpy as jnp
from jax import lax
from jax.experimental import pallas as pl
from jax.experimental.pallas import tpu as pltpu
from jax.sharding import PartitionSpec as P

MESH = pl.DeviceIdType.MESH
EXPERTS = 8
MOST = 18
TOK = 128
D = 2048
NX, NY, NZ = 4, 8, 8
HALF_HID = 96
WROWS = 3 * HALF_HID
GU = 2 * HALF_HID
BLK = D // NY
ROWS = EXPERTS * MOST
SEND = 48
BACK = 32
F32 = jnp.float32
BF16 = jnp.bfloat16
NT = (((1,), (1,)), ((), ()))
TN = (((0,), (0,)), ((), ()))
NN = (((1,), (0,)), ((), ()))


def dot(a, b, dims=NN):
    return lax.dot_general(a, b, dims, preferred_element_type=F32)


def iota(shape, dim):
    return lax.broadcasted_iota(jnp.int32, shape, dim)


def pick(cond):
    return jnp.where(cond, 1.0, 0.0).astype(BF16)


def kernel(
    routes, gates, tok, cot, gp, up, dn, gin, grads,
    xd, wall, rcv, xs, ds, gr, rb, tot, zb, dxp, dxr, ret, dgu,
    disp_s, disp_r, loc, sib_s, sib_r, wz_s, wz_r, ag_s, ag_r,
    dx_s, dx_r, ret_s, ret_r, rs_s, rs_r, zs_s, zs_r,
):
    di, ei = lax.axis_index("dp"), lax.axis_index("expert")
    y, c = di // 2, di % 2
    x, z = ei // NZ, ei % NZ
    h, zl = z // 4, z % 4
    sibling = {"dp": y * 2 + (1 - c), "expert": ei}
    above = {"dp": ((y + 1) % NY) * 2 + c, "expert": ei}
    below = {"dp": ((y + NY - 1) % NY) * 2 + c, "expert": ei}

    def at_x(dx, rel):
        return ((x + dx) % NX) * NZ + (z if rel == 0 else NZ - 1 - z)

    def at_z(q, core=None):
        dp = di if core is None else y * 2 + core
        return {"dp": dp, "expert": x * NZ + h * 4 + (zl + q) % 4}

    far = [(dx, rel) for rel in (0, 1) for dx in range(NX) if dx or rel]

    def remote(src, dst, send, recv, where):
        return pltpu.make_async_remote_copy(
            src_ref=src, dst_ref=dst, send_sem=send, recv_sem=recv,
            device_id=where, device_id_type=MESH,
        )

    barrier = pltpu.get_barrier_semaphore()
    partners = [sibling, above, below]
    partners += [{"dp": di, "expert": at_x(dx, rel)} for dx, rel in far]
    partners += [at_z(q, core) for q in (1, 2, 3) for core in (0, 1)]
    for p in partners:
        pl.semaphore_signal(barrier, inc=1, device_id=p, device_id_type=MESH)

    mine = pick(iota((HALF_HID, GU), 1) == iota((HALF_HID, GU), 0) + c * HALF_HID)

    def own_block(b):
        at = pl.multiple_of(b * BLK, BLK)
        wall[0, b, 0:HALF_HID, :] = dot(mine, gp[pl.ds(at, BLK), :], NT).astype(BF16)
        wall[0, b, HALF_HID:GU, :] = dot(mine, up[pl.ds(at, BLK), :], NT).astype(BF16)
        wall[0, b, GU:WROWS, :] = dot(mine, dn[:, pl.ds(at, BLK)]).astype(BF16)

    own_block(y)
    pl.semaphore_wait(barrier, len(partners))

    wz = [
        remote(wall.at[0, y], wall.at[q, y], wz_s.at[q - 1], wz_r.at[q - 1], at_z(q))
        for q in (1, 2, 3)
    ]
    for w in wz:
        w.start()

    route = routes[...]
    one_hot = pick(iota((TOK, 128), 1) == route)
    earlier = pick(iota((TOK, TOK), 0) > iota((TOK, TOK), 1))
    rank = jnp.sum(dot(earlier, one_hot) * one_hot.astype(F32), axis=1, keepdims=True)
    rank = rank.astype(jnp.int32)
    lanes = iota((TOK, EXPERTS * SEND), 1)
    first = route * SEND + rank
    place = jnp.concatenate([pick(lanes == first), pick(lanes == first + 24)], axis=0)
    weight = gates[...]
    for b in range(4):
        cols = slice(b * 512, b * 512 + 512)
        scaled = (cot[:, cols].astype(F32) * weight).astype(BF16)
        both = jnp.concatenate([tok[:, cols], scaled], axis=0)
        xd[:, cols] = dot(place, both, TN).astype(BF16)

    def rows_of(e, n):
        return pl.ds(pl.multiple_of(e * n, n), n)

    sends = []
    for i, (dx, rel) in enumerate(far):
        e = ((x + dx) % NX) * 2 + (h if rel == 0 else 1 - h)
        sends.append(
            remote(
                xd.at[rows_of(e, SEND)], rcv.at[c, rows_of(x * 2 + rel, SEND)],
                disp_s.at[i], disp_r.at[i], {"dp": di, "expert": at_x(dx, rel)},
            )
        )
        sends[-1].start()
    keep = pltpu.make_async_copy(
        xd.at[rows_of(x * 2 + h, SEND)], rcv.at[c, rows_of(x * 2, SEND)], loc
    )
    keep.start()

    def ag(way, t, q):
        b = (y - t + NY) % NY if way == 0 else (y + t) % NY
        ref = wall.at[q, b]
        if t == 3:
            ref = wall.at[q, b, pl.ds(way * (WROWS // 2), WROWS // 2)]
        return remote(
            ref, ref, ag_s.at[way, t, q - 1], ag_r.at[way, t, q - 1],
            above if way == 0 else below,
        )

    def ag_in(way, t, q):
        b = (y - 1 - t + NY) % NY if way == 0 else (y + 1 + t) % NY
        ref = wall.at[q, b]
        if t == 3:
            ref = wall.at[q, b, pl.ds(way * (WROWS // 2), WROWS // 2)]
        remote(
            ref, ref, ag_s.at[way, t, q - 1], ag_r.at[way, t, q - 1],
            above if way == 0 else below,
        ).wait_recv()

    for q in (1, 2, 3):
        wz[q - 1].wait_recv()
        for way in (0, 1):
            ag(way, 0, q).start()
    for k in range(1, NY):
        own_block((y + k) % NY)

    for t in (1, 2):
        for q in (1, 2, 3):
            for way in (0, 1):
                ag_in(way, t - 1, q)
                ag(way, t, q).start()

    def to_sibling(i, dx, rel):
        ref = rcv.at[c, rows_of(((x - dx + NX) % NX) * 2 + rel, SEND)]
        return remote(ref, ref, sib_s.at[i], sib_r.at[i], sibling)

    def from_sibling(i, dx, rel):
        ref = rcv.at[1 - c, rows_of(((x - dx + NX) % NX) * 2 + rel, SEND)]
        return remote(ref, ref, sib_s.at[i], sib_r.at[i], sibling)

    keep.wait()
    to_sibling(7, 0, 0).start()
    for i, (dx, rel) in enumerate(far):
        sends[i].wait_recv()
        to_sibling(i, dx, rel).start()

    for q in (1, 2, 3):
        for way in (0, 1):
            ag_in(way, 2, q)
            ag(way, 3, q).start()

    for i, (dx, rel) in enumerate(far + [(0, 0)]):
        from_sibling(i, dx, rel).wait_recv()

    row = iota((ROWS, EXPERTS * SEND), 0)
    for m in range(1, EXPERTS):
        row = row + jnp.where(iota((ROWS, EXPERTS * SEND), 0) >= MOST * m, SEND - MOST, 0)
    col = iota((ROWS, EXPERTS * SEND), 1)
    sel_x, sel_d = pick(col == row), pick(col == row + 24)
    for core in (0, 1):
        for b in range(4):
            cols = slice(b * 512, b * 512 + 512)
            part = rcv[core, :, cols]
            xs[core * ROWS:core * ROWS + ROWS, cols] = dot(sel_x, part).astype(BF16)
            ds[core * ROWS:core * ROWS + ROWS, cols] = dot(sel_d, part).astype(BF16)

    def rs(way, t, s):
        if t == 0:
            half = pl.ds(way * (WROWS // 2), WROWS // 2)
            src, dst = gr.at[s, (y + 4) % NY, half], rb.at[way, 0, s, half]
        else:
            src, dst = rb.at[way, t - 1, s], rb.at[way, t, s]
        return remote(
            src, dst, rs_s.at[way, t, s], rs_r.at[way, t, s],
            above if way == 0 else below,
        )

    def compute(s):
        pre = jnp.zeros((GU, 2 * ROWS), F32)
        dh = jnp.zeros((HALF_HID, 2 * ROWS), F32)
        for b in range(NY):
            cols = slice(b * BLK, b * BLK + BLK)
            pre = pre + dot(wall[s, b, 0:GU, :], xs[:, cols], NT)
            dh = dh + dot(wall[s, b, GU:WROWS, :], ds[:, cols], NT)
        g, u = pre[0:HALF_HID], pre[HALF_HID:GU]
        sig = 1.0 / (1.0 + jnp.exp(-g))
        hid = (g * sig * u).astype(BF16)
        d_gate = (dh * u * sig * (1.0 + g * (1.0 - sig))).astype(BF16)
        d_up = (dh * g * sig).astype(BF16)
        dboth = jnp.concatenate([d_gate, d_up], axis=0)
        dgu[s * GU:s * GU + GU, :] = dboth
        for k in range(NY):
            b = k
            cols = slice(b * BLK, b * BLK + BLK)
            gr[s, b, 0:GU, :] = dot(dboth, xs[:, cols]).astype(BF16)
            gr[s, b, GU:WROWS, :] = dot(hid, ds[:, cols]).astype(BF16)

    for s in range(4):
        if s:
            for way in (0, 1):
                ag_in(way, 3, s)
        compute(s)
        for way in (0, 1):
            rs(way, 0, s).start()

    j, i_ = iota((EXPERTS * BACK, ROWS), 0), iota((EXPERTS * BACK, ROWS), 1)
    spread = pick((i_ == j - (BACK - MOST) * (j // BACK)) & (j % BACK < MOST))
    for b in range(NY):
        cols = slice(b * BLK, b * BLK + BLK)
        rhs = jnp.concatenate([wall[s, b, 0:GU, :] for s in range(4)], axis=0)
        dx = dot(dgu[...], rhs, TN).astype(BF16)
        for core in (0, 1):
            dxp[core, :, cols] = dot(spread, dx[core * ROWS:core * ROWS + ROWS]).astype(BF16)
    dx_out = remote(dxp.at[1 - c], dxr, dx_s, dx_r, sibling)
    dx_out.start()

    def rs_add(way, t, s):
        rs(way, t, s).wait_recv()
        b = (y + 3 - t) % NY if way == 0 else (y - 3 + t + NY) % NY
        if t == 0:
            lo, hi = way * (WROWS // 2), (1 - way) * (WROWS // 2)
            a, o = pl.ds(lo, WROWS // 2), pl.ds(hi, WROWS // 2)
            rb[way, 0, s, a, :] = (rb[way, 0, s, a, :].astype(F32) + gr[s, b, a, :].astype(F32)).astype(BF16)
            rb[way, 0, s, o, :] = gr[s, b, o, :]
        else:
            rb[way, t, s] = (rb[way, t, s].astype(F32) + gr[s, b].astype(F32)).astype(BF16)

    for t in (0, 1, 2):
        for s in range(4):
            for way in (0, 1):
                rs_add(way, t, s)
                rs(way, t + 1, s).start()
        if t == 0:
            dx_out.wait_recv()
            dxr[...] = (dxr[...].astype(F32) + dxp[c].astype(F32)).astype(BF16)
            backs = []
            for i, (dx, rel) in enumerate(far):
                slot = ((x + dx) % NX) * 2 + rel
                backs.append(
                    remote(
                        dxr.at[rows_of(slot, BACK)], ret.at[rows_of(x * 2 + h, BACK)],
                        ret_s.at[i], ret_r.at[i], {"dp": di, "expert": at_x(dx, rel)},
                    )
                )
                backs[-1].start()
            back_own = pltpu.make_async_copy(
                dxr.at[rows_of(x * 2, BACK)], ret.at[rows_of(x * 2 + h, BACK)], loc
            )
            back_own.start()

    finals = []
    for s in range(4):
        for way in (0, 1):
            rs(way, 3, s).wait_recv()
        total = gr[s, y].astype(F32) + rb[0, 3, s].astype(F32) + rb[1, 3, s].astype(F32)
        for core in (0, 1):
            tot[s, core] = total[:, core * 128:core * 128 + 128].astype(BF16)
        if s:
            for core in (0, 1):
                k = 2 * s - 1 + core
                finals.append(
                    remote(tot.at[s, core], zb.at[s, c], zs_s.at[k], zs_r.at[s, c], at_z(4 - s, core))
                )
                finals[-1].start()
        else:
            finals.append(remote(tot.at[0, 1 - c], zb.at[0, c], zs_s.at[0], zs_r.at[0, c], sibling))
            finals[-1].start()
            zb[0, c] = tot[0, c]

    back_own.wait()
    for b in backs:
        b.wait_recv()
    take = pick(iota((TOK, EXPERTS * BACK), 1) == route * BACK + rank)
    for b in range(4):
        cols = slice(b * 512, b * 512 + 512)
        gin[:, cols] = dot(take, ret[:, cols]).astype(BF16)

    remote(tot.at[0, c], zb.at[0, 1 - c], zs_s.at[0], zs_r.at[0, 1 - c], sibling).wait_recv()
    for s in (1, 2, 3):
        for core in (0, 1):
            remote(tot.at[s, core], zb.at[s, core], zs_s.at[0], zs_r.at[s, core], sibling).wait_recv()
    for core in (0, 1):
        acc = zb[0, core].astype(F32) + zb[1, core].astype(F32)
        grads[core] = acc + (zb[2, core].astype(F32) + zb[3, core].astype(F32))

    for w in wz + sends + finals + backs + [dx_out]:
        w.wait_send()
    for i, (dx, rel) in enumerate(far + [(0, 0)]):
        to_sibling(i, dx, rel).wait_send()
    for way in (0, 1):
        for t in range(4):
            for q in (1, 2, 3):
                ag(way, t, q).wait_send()
            for s in range(4):
                rs(way, t, s).wait_send()


def body(tokens, cotangent, routes, expert_gates, gate_proj, up_proj, down_proj):
    vmem = pl.BlockSpec(memory_space=pltpu.VMEM)
    dma = pltpu.SemaphoreType.DMA
    gin, grads = pl.pallas_call(
        kernel,
        out_shape=(
            jax.ShapeDtypeStruct((TOK, D), BF16),
            jax.ShapeDtypeStruct((2, WROWS, 128), F32),
        ),
        in_specs=[vmem] * 7,
        out_specs=(vmem, vmem),
        scratch_shapes=[
            pltpu.VMEM((EXPERTS * SEND, D), BF16),
            pltpu.VMEM((4, NY, WROWS, BLK), BF16),
            pltpu.VMEM((2, EXPERTS * SEND, D), BF16),
            pltpu.VMEM((2 * ROWS, D), BF16),
            pltpu.VMEM((2 * ROWS, D), BF16),
            pltpu.VMEM((4, NY, WROWS, BLK), BF16),
            pltpu.VMEM((2, 4, 4, WROWS, BLK), BF16),
            pltpu.VMEM((4, 2, WROWS, 128), BF16),
            pltpu.VMEM((4, 2, WROWS, 128), BF16),
            pltpu.VMEM((2, EXPERTS * BACK, D), BF16),
            pltpu.VMEM((EXPERTS * BACK, D), BF16),
            pltpu.VMEM((EXPERTS * BACK, D), BF16),
            pltpu.VMEM((4 * GU, 2 * ROWS), BF16),
            dma((7,)), dma((7,)), dma, dma((8,)), dma((8,)), dma((3,)), dma((3,)),
            dma((2, 4, 3)), dma((2, 4, 3)), dma, dma, dma((7,)), dma((7,)),
            dma((2, 4, 4)), dma((2, 4, 4)), dma((7,)), dma((4, 2)),
        ],
        compiler_params=pltpu.CompilerParams(
            collective_id=0, has_side_effects=True, vmem_limit_bytes=56 * 2**20
        ),
    )(routes, expert_gates, tokens, cotangent, gate_proj, up_proj, down_proj)
    parts = jnp.concatenate([grads[0].reshape(3, HALF_HID, 128), grads[1].reshape(3, HALF_HID, 128)], axis=1)
    return gin, parts[0].T, parts[1].T, parts[2]


def solution(mesh):
    in_specs = (
        P(("dp", "expert"), None),
        P(("dp", "expert"), None),
        P(("dp", "expert"), None),
        P(("dp", "expert"), None),
        P(None, "expert"),
        P(None, "expert"),
        P("expert", None),
    )
    out_specs = (P(("dp", "expert"), None), P("dp", "expert"), P("dp", "expert"), P("expert", "dp"))
    return jax.shard_map(body, mesh=mesh, in_specs=in_specs, out_specs=out_specs, check_vma=False)
```

```python
import jax
import jax.numpy as jnp
from jax import lax
from jax.experimental import pallas as pl
from jax.experimental.pallas import tpu as pltpu
from jax.sharding import PartitionSpec as P

MESH = pl.DeviceIdType.MESH
EXPERTS = 8
MOST = 18
TOK = 128
D = 2048
NX, NY, NZ = 4, 8, 8
HALF_HID = 96
WROWS = 3 * HALF_HID
GU = 2 * HALF_HID
BLK = D // NY
ROWS = EXPERTS * MOST
WIDE = 512
MSG = 144
F32 = jnp.float32
BF16 = jnp.bfloat16
NT = (((1,), (1,)), ((), ()))
TN = (((0,), (0,)), ((), ()))
NN = (((1,), (0,)), ((), ()))


def dot(a, b, dims=NN):
    return lax.dot_general(a, b, dims, preferred_element_type=F32)


def iota(shape, dim):
    return lax.broadcasted_iota(jnp.int32, shape, dim)


def pick(cond):
    return jnp.where(cond, 1.0, 0.0).astype(BF16)


def packed(ref, lead, start, size):
    parts = [ref[(*lead, slice(k * MSG + start, k * MSG + start + size))] for k in range(EXPERTS)]
    parts += [ref[(*lead, slice(k * MSG + 128, k * MSG + MSG))] for k in range(EXPERTS)]
    return jnp.concatenate(parts, axis=0)


def kernel(
    routes, gates, tok, cot, gp, up, dn, gin, g_out, u_out, d_out,
    xd, wall, rcv, xs, ds, gr, rb, tot, zb, dxp, dxr, dxn, ret, dgu, hid,
    own_s, disp_s, disp_r, loc, nb_s, nb_r, sib_s, sib_r, wz_s, wz_r, ag_s, ag_r,
    dx_s, dx_r, dn_s, dn_r, ret_s, ret_r, rs_s, rs_r, zs_s, zs_r,
):
    di, ei = lax.axis_index("dp"), lax.axis_index("expert")
    y, c = di // 2, di % 2
    x, z = ei // NZ, ei % NZ
    h, zl = z // 4, z % 4
    sibling = {"dp": y * 2 + (1 - c), "expert": ei}
    above = {"dp": ((y + 1) % NY) * 2 + c, "expert": ei}
    below = {"dp": ((y + NY - 1) % NY) * 2 + c, "expert": ei}
    beside = {"dp": di, "expert": x * NZ + z + 1 - 2 * (z % 2)}

    def at_x(dx, rel):
        return ((x + dx) % NX) * NZ + (z if rel == 0 else NZ - 1 - z)

    def mirror(core):
        return {"dp": y * 2 + core, "expert": x * NZ + h * 4 + 3 - zl}

    far = [(dx, 1) for dx in (0, 1, 3, 2)] + [(dx, 0) for dx in (1, 3, 2)]

    def remote(src, dst, send, recv, where):
        return pltpu.make_async_remote_copy(
            src_ref=src, dst_ref=dst, send_sem=send, recv_sem=recv,
            device_id=where, device_id_type=MESH,
        )

    barrier = pltpu.get_barrier_semaphore()
    partners = [sibling, above, below, beside, mirror(0), mirror(1)]
    partners += [{"dp": di, "expert": at_x(dx, rel)} for dx, rel in far]
    for p in partners:
        pl.semaphore_signal(barrier, inc=1, device_id=p, device_id_type=MESH)

    half_hid = pl.ds(pl.multiple_of(c * HALF_HID, HALF_HID), HALF_HID)

    def own_block(b):
        cols = pl.ds(pl.multiple_of(b * BLK, BLK), BLK)
        return [
            pltpu.make_async_copy(
                w.at[half_hid, cols], wall.at[0, b, pl.ds(m * HALF_HID, HALF_HID)], own_s.at[b, m]
            )
            for m, w in enumerate((gp, up, dn))
        ]

    for k in range(NY):
        for w in own_block((y + k) % NY):
            w.start()

    route = routes[...]
    one_hot = pick(iota((16, TOK), 0) == route)
    earlier = pick(iota((TOK, TOK), 0) < iota((TOK, TOK), 1))
    rank = jnp.sum(dot(one_hot, earlier) * one_hot.astype(F32), axis=0, keepdims=True)
    rank = rank.astype(jnp.int32)
    low = rank < 16
    slots = iota((EXPERTS * 32, TOK), 0)
    main = jnp.where(low, route * 32 + rank, -1)
    place = jnp.concatenate(
        [pick(slots == main), pick(slots == jnp.where(low, main + 16, -1))], axis=1
    )
    slots = iota((EXPERTS * 16, TOK), 0)
    diagonal = iota((TOK, TOK), 0) == iota((TOK, TOK), 1)
    weight = jnp.sum(jnp.where(diagonal, gates[...], 0.0), axis=1, keepdims=True)
    rest = jnp.zeros((EXPERTS * 16, WIDE), F32)
    for b in range(4):
        cols = slice(b * WIDE, b * WIDE + WIDE)
        scaled = (cot[:, cols].astype(F32) * weight).astype(BF16)
        both = jnp.concatenate([tok[:, cols], scaled], axis=0)
        out = dot(place, both).astype(BF16)
        over = jnp.where(low, -1, route * 16 + 4 * b + rank - 16)
        over = jnp.concatenate(
            [pick(slots == over), pick(slots == jnp.where(low, -1, over + 2))], axis=1
        )
        rest = rest + dot(over, both)
        for e in range(EXPERTS):
            xd[e * MSG + b * 32:e * MSG + b * 32 + 32] = out[e * 32:e * 32 + 32]
    rest = rest.astype(BF16)
    for e in range(EXPERTS):
        xd[e * MSG + 128:e * MSG + MSG] = rest[e * 16:e * 16 + 16]

    for w in own_block(y):
        w.wait()
    pl.semaphore_wait(barrier, len(partners))
    wz = remote(wall.at[0, y], wall.at[1, y], wz_s, wz_r, mirror(c))
    wz.start()

    def msg(e):
        return pl.ds(pl.multiple_of(e * MSG, MSG), MSG)

    sends = []
    for i, (dx, rel) in enumerate(far):
        e = ((x + dx) % NX) * 2 + (h if rel == 0 else 1 - h)
        sends.append(
            remote(
                xd.at[msg(e)], rcv.at[c, msg(x * 2 + rel)],
                disp_s.at[i], disp_r.at[i], {"dp": di, "expert": at_x(dx, rel)},
            )
        )
        sends[-1].start()
    keep = pltpu.make_async_copy(xd.at[msg(x * 2 + h)], rcv.at[c, msg(x * 2)], loc)
    keep.start()

    def slot(i):
        dx, rel = (far + [(0, 0)])[i]
        return msg(((x - dx + NX) % NX) * 2 + rel)

    def to_beside(i):
        return remote(
            rcv.at[c, slot(i)], rcv.at[2 + c, slot(i)], nb_s.at[i], nb_r.at[i], beside
        )

    def from_beside(i):
        return remote(rcv.at[c, slot(i)], rcv.at[2 + c, slot(i)], nb_s.at[i], nb_r.at[i], beside)

    def to_sibling(n, i):
        ref = rcv.at[2 * n + c, slot(i)]
        return remote(ref, ref, sib_s.at[n, i], sib_r.at[n, i], sibling)

    def from_sibling(n, i):
        ref = rcv.at[2 * n + 1 - c, slot(i)]
        return remote(ref, ref, sib_s.at[n, i], sib_r.at[n, i], sibling)

    def ag(way, t):
        b = (y - t + NY) % NY if way == 0 else (y + t) % NY
        ref = wall.at[1, b]
        if t == 3:
            ref = wall.at[1, b, pl.ds(way * (WROWS // 2), WROWS // 2)]
        return remote(ref, ref, ag_s.at[way, t], ag_r.at[way, t], above if way == 0 else below)

    def ag_in(way, t):
        b = (y - 1 - t + NY) % NY if way == 0 else (y + 1 + t) % NY
        ref = wall.at[1, b]
        if t == 3:
            ref = wall.at[1, b, pl.ds(way * (WROWS // 2), WROWS // 2)]
        remote(ref, ref, ag_s.at[way, t], ag_r.at[way, t], above if way == 0 else below).wait_recv()

    def ag_step(t):
        for way in (0, 1):
            ag_in(way, t - 1)
            ag(way, t).start()

    def forward(i):
        if i < 7:
            sends[i].wait_recv()
        else:
            keep.wait()
        to_beside(i).start()
        to_sibling(0, i).start()

    def forward_beside(i):
        from_beside(i).wait_recv()
        to_sibling(1, i).start()

    forward(7)
    wz.wait_recv()
    for way in (0, 1):
        ag(way, 0).start()
    for i in (4, 5, 6):
        forward(i)
    ag_step(1)
    for i in (0, 1):
        forward(i)
    ag_step(2)
    for i in (2, 3):
        forward(i)
    for i in (7, 4, 5, 6):
        forward_beside(i)
    ag_step(3)
    for k in range(1, NY):
        for w in own_block((y + k) % NY):
            w.wait()
    for i in (0, 1, 2, 3):
        forward_beside(i)

    row = iota((ROWS, 1), 0)
    source = jnp.zeros((ROWS, 1), jnp.int32)
    for m in range(1, EXPERTS):
        source = source + jnp.where(row >= MOST * m, 1, 0)
    row = row - MOST * source
    col = iota((ROWS, EXPERTS * 48), 1)

    def gather_rows(n, core):
        part = 2 * n + core
        at = slice(part * ROWS, part * ROWS + ROWS)
        for b in range(4):
            cols = slice(b * WIDE, b * WIDE + WIDE)
            sel_x = pick(col == jnp.where(row < 16, source * 32 + row, 240 + source * 16 + 4 * b + row))
            sel_d = pick(col == jnp.where(row < 16, source * 32 + 16 + row, 242 + source * 16 + 4 * b + row))
            rows = packed(rcv, (part,), b * 32, 32)
            xs[at, cols] = dot(sel_x, rows).astype(BF16)
            ds[at, cols] = dot(sel_d, rows).astype(BF16)

    for n in (0, 1):
        for i in range(8):
            from_sibling(n, i).wait_recv()
        for core in (0, 1):
            gather_rows(n, core)

    def rs(way, t, s):
        if t == 0:
            half = pl.ds(way * (WROWS // 2), WROWS // 2)
            src, dst = gr.at[s, (y + 4) % NY, half], rb.at[way, 0, s, half]
        else:
            src, dst = rb.at[way, t - 1, s], rb.at[way, t, s]
        return remote(
            src, dst, rs_s.at[way, t, s], rs_r.at[way, t, s], above if way == 0 else below
        )

    def activations(s):
        pre = jnp.zeros((GU, 4 * ROWS), F32)
        dh = jnp.zeros((HALF_HID, 4 * ROWS), F32)
        for b in range(NY):
            cols = slice(b * BLK, b * BLK + BLK)
            pre = pre + dot(wall[s, b, 0:GU, :], xs[:, cols], NT)
            dh = dh + dot(wall[s, b, GU:WROWS, :], ds[:, cols], NT)
        g, u = pre[0:HALF_HID], pre[HALF_HID:GU]
        sig = 1.0 / (1.0 + jnp.exp(-g))
        hid[s * HALF_HID:s * HALF_HID + HALF_HID] = (g * sig * u).astype(BF16)
        dgu[s * GU:s * GU + HALF_HID] = (dh * u * sig * (1.0 + g * (1.0 - sig))).astype(BF16)
        dgu[s * GU + HALF_HID:s * GU + GU] = (dh * g * sig).astype(BF16)

    def weight_grads(s):
        for b in range(NY):
            cols = slice(b * BLK, b * BLK + BLK)
            gr[s, b, 0:GU, :] = dot(dgu[s * GU:s * GU + GU], xs[:, cols]).astype(BF16)
            gr[s, b, GU:WROWS, :] = dot(hid[s * HALF_HID:s * HALF_HID + HALF_HID], ds[:, cols]).astype(BF16)
        for way in (0, 1):
            rs(way, 0, s).start()

    activations(0)
    weight_grads(0)
    for way in (0, 1):
        ag_in(way, 3)
    activations(1)

    j, i_ = iota((EXPERTS * 16, ROWS), 0), iota((EXPERTS * 16, ROWS), 1)
    spread = pick(i_ == j + 2 * (j // 16))
    lasts = [jnp.zeros((EXPERTS * 16, BLK), F32) for _ in range(4)]
    for b in range(NY):
        cols = slice(b * BLK, b * BLK + BLK)
        rhs = jnp.concatenate([wall[s, b, 0:GU, :] for s in (0, 1)], axis=0)
        dx = dot(dgu[...], rhs, TN).astype(BF16)
        own = j % 16 - 2 * b
        spread_last = pick((i_ == MOST * (j // 16) + 16 + own) & (own >= 0) & (own < 2))
        for part in range(4):
            mine = dx[part * ROWS:part * ROWS + ROWS]
            out = dot(spread, mine).astype(BF16)
            lasts[part] = lasts[part] + dot(spread_last, mine)
            for k in range(EXPERTS):
                dxp[part, k * MSG + b * 16:k * MSG + b * 16 + 16] = out[k * 16:k * 16 + 16]
    for part in range(4):
        last = lasts[part].astype(BF16)
        for k in range(EXPERTS):
            dxp[part, k * MSG + 128:k * MSG + MSG] = last[k * 16:k * 16 + 16]

    dx_out = [
        remote(dxp.at[2 * n + 1 - c], dxr.at[n], dx_s.at[n], dx_r.at[n], sibling) for n in (0, 1)
    ]
    for n in (1, 0):
        dx_out[n].start()
    weight_grads(1)

    def rs_add(way, t, s):
        rs(way, t, s).wait_recv()
        b = (y + 3 - t) % NY if way == 0 else (y - 3 + t + NY) % NY
        if t == 0:
            lo, hi = way * (WROWS // 2), (1 - way) * (WROWS // 2)
            a, o = pl.ds(lo, WROWS // 2), pl.ds(hi, WROWS // 2)
            rb[way, 0, s, a, :] = (rb[way, 0, s, a, :].astype(F32) + gr[s, b, a, :].astype(F32)).astype(BF16)
            rb[way, 0, s, o, :] = gr[s, b, o, :]
        else:
            rb[way, t, s] = (rb[way, t, s].astype(F32) + gr[s, b].astype(F32)).astype(BF16)

    def rs_step(t, s):
        for way in (0, 1):
            rs_add(way, t, s)
            rs(way, t + 1, s).start()

    dx_beside = remote(dxr.at[1], dxn, dn_s, dn_r, beside)
    dx_out[1].wait_recv()
    dxr[1] = (dxr[1].astype(F32) + dxp[2 + c].astype(F32)).astype(BF16)
    dx_beside.start()
    for s in (0, 1):
        rs_step(0, s)
    dx_out[0].wait_recv()
    for s in (0, 1):
        rs_step(1, s)
    dx_beside.wait_recv()
    dxr[0] = (dxr[0].astype(F32) + dxp[c].astype(F32) + dxn[...].astype(F32)).astype(BF16)
    backs = []
    for i, (dx, rel) in enumerate(far):
        backs.append(
            remote(
                dxr.at[0, msg(((x + dx) % NX) * 2 + rel)], ret.at[msg(x * 2 + h)],
                ret_s.at[i], ret_r.at[i], {"dp": di, "expert": at_x(dx, rel)},
            )
        )
        backs[-1].start()
    back_own = pltpu.make_async_copy(dxr.at[0, msg(x * 2)], ret.at[msg(x * 2 + h)], loc)
    back_own.start()
    for s in (1, 0):
        rs_step(2, s)

    finals = []
    for s in (1, 0):
        for way in (0, 1):
            rs(way, 3, s).wait_recv()
        total = gr[s, y].astype(F32) + rb[0, 3, s].astype(F32) + rb[1, 3, s].astype(F32)
        for core in (0, 1):
            tot[s, core] = total[:, core * 128:core * 128 + 128].astype(BF16)
        if s:
            for core in (0, 1):
                finals.append(
                    remote(tot.at[1, core], zb.at[1, c], zs_s.at[core], zs_r.at[1, c], mirror(core))
                )
                finals[-1].start()
        else:
            finals.append(remote(tot.at[0, 1 - c], zb.at[0, c], zs_s.at[2], zs_r.at[0, c], sibling))
            finals[-1].start()
            zb[0, c] = tot[0, c]

    back_own.wait()
    for b in backs:
        b.wait_recv()

    def column(row):
        held = jnp.sum(jnp.where(diagonal, row.astype(F32), 0.0), axis=1, keepdims=True)
        return held.astype(jnp.int32)

    route, rank = column(route), column(rank)
    cols_of = iota((TOK, EXPERTS * 32), 1)
    for b in range(NY):
        at = jnp.where(rank < 16, route * 16 + rank, 112 + route * 16 + 2 * b + rank)
        take = pick(cols_of == at)
        gin[:, b * BLK:b * BLK + BLK] = dot(take, packed(ret, (), b * 16, 16)).astype(BF16)

    remote(tot.at[0, c], zb.at[0, 1 - c], zs_s.at[0], zs_r.at[0, 1 - c], sibling).wait_recv()
    for core in (0, 1):
        remote(tot.at[1, core], zb.at[1, core], zs_s.at[0], zs_r.at[1, core], sibling).wait_recv()
    for core in (0, 1):
        acc = zb[0, core].astype(F32) + zb[1, core].astype(F32)
        for m, out in enumerate((g_out, u_out, d_out)):
            out[core * HALF_HID:(core + 1) * HALF_HID] = acc[m * HALF_HID:(m + 1) * HALF_HID]

    for w in [wz] + sends + finals + backs + dx_out + [dx_beside]:
        w.wait_send()
    for i in range(8):
        to_beside(i).wait_send()
        for n in (0, 1):
            to_sibling(n, i).wait_send()
    for way in (0, 1):
        for t in range(4):
            ag(way, t).wait_send()
            for s in (0, 1):
                rs(way, t, s).wait_send()


def body(tokens, cotangent, routes, expert_gates, gate_proj, up_proj, down_proj):
    vmem = pl.BlockSpec(memory_space=pltpu.VMEM)
    dma = pltpu.SemaphoreType.DMA
    anywhere = pl.BlockSpec(memory_space=pl.ANY)
    gin, g_t, u_t, d_g = pl.pallas_call(
        kernel,
        out_shape=(
            jax.ShapeDtypeStruct((TOK, D), BF16),
            jax.ShapeDtypeStruct((GU, 128), F32),
            jax.ShapeDtypeStruct((GU, 128), F32),
            jax.ShapeDtypeStruct((GU, 128), F32),
        ),
        in_specs=[vmem] * 4 + [anywhere] * 3,
        out_specs=(vmem,) * 4,
        scratch_shapes=[
            pltpu.VMEM((EXPERTS * MSG, WIDE), BF16),
            pltpu.VMEM((2, NY, WROWS, BLK), BF16),
            pltpu.VMEM((4, EXPERTS * MSG, WIDE), BF16),
            pltpu.VMEM((4 * ROWS, D), BF16),
            pltpu.VMEM((4 * ROWS, D), BF16),
            pltpu.VMEM((2, NY, WROWS, BLK), BF16),
            pltpu.VMEM((2, 4, 2, WROWS, BLK), BF16),
            pltpu.VMEM((2, 2, WROWS, 128), BF16),
            pltpu.VMEM((2, 2, WROWS, 128), BF16),
            pltpu.VMEM((4, EXPERTS * MSG, BLK), BF16),
            pltpu.VMEM((2, EXPERTS * MSG, BLK), BF16),
            pltpu.VMEM((EXPERTS * MSG, BLK), BF16),
            pltpu.VMEM((EXPERTS * MSG, BLK), BF16),
            pltpu.VMEM((2 * GU, 4 * ROWS), BF16),
            pltpu.VMEM((2 * HALF_HID, 4 * ROWS), BF16),
            dma((NY, 3)), dma((7,)), dma((7,)), dma, dma((8,)), dma((8,)), dma((2, 8)), dma((2, 8)),
            dma, dma, dma((2, 4)), dma((2, 4)), dma((2,)), dma((2,)), dma, dma,
            dma((7,)), dma((7,)), dma((2, 4, 2)), dma((2, 4, 2)), dma((3,)), dma((2, 2)),
        ],
        compiler_params=pltpu.CompilerParams(
            collective_id=0, has_side_effects=True, vmem_limit_bytes=56 * 2**20
        ),
    )(
        routes.reshape(1, TOK), expert_gates.reshape(1, TOK), tokens, cotangent,
        gate_proj.T, up_proj.T, down_proj,
    )
    return gin, g_t.T, u_t.T, d_g


def solution(mesh):
    in_specs = (
        P(("dp", "expert"), None),
        P(("dp", "expert"), None),
        P(("dp", "expert"), None),
        P(("dp", "expert"), None),
        P(None, "expert"),
        P(None, "expert"),
        P("expert", None),
    )
    out_specs = (P(("dp", "expert"), None), P("dp", "expert"), P("dp", "expert"), P("expert", "dp"))
    return jax.shard_map(body, mesh=mesh, in_specs=in_specs, out_specs=out_specs, check_vma=False)
```

```python
import jax
import jax.numpy as jnp
from jax import lax
from jax.experimental import pallas as pl
from jax.experimental.pallas import tpu as pltpu
from jax.sharding import PartitionSpec as P

MESH = pl.DeviceIdType.MESH
EXPERTS = 8
MOST = 18
TOK = 128
D = 2048
NX, NY, NZ = 4, 8, 8
HALF_HID = 96
WROWS = 3 * HALF_HID
GU = 2 * HALF_HID
BLK = D // NY
ROWS = EXPERTS * MOST
WIDE = 512
MSG = 144
F32 = jnp.float32
BF16 = jnp.bfloat16
NT = (((1,), (1,)), ((), ()))
TN = (((0,), (0,)), ((), ()))
NN = (((1,), (0,)), ((), ()))


def dot(a, b, dims=NN):
    return lax.dot_general(a, b, dims, preferred_element_type=F32)


def iota(shape, dim):
    return lax.broadcasted_iota(jnp.int32, shape, dim)


def pick(cond):
    return jnp.where(cond, 1.0, 0.0).astype(BF16)


def packed(messages, start, size):
    parts = [ref[(*lead, slice(at + start, at + start + size))] for ref, lead, at in messages]
    parts += [ref[(*lead, slice(at + 128, at + MSG))] for ref, lead, at in messages]
    return jnp.concatenate(parts, axis=0)


def kernel(
    routes, gates, tok, cot, gp, up, dn, gin, grads,
    xd, wall, rcv, xs, ds, gr, rb, tot, zb, dxp, dxr, dxn, ret, dgu, hid,
    own_s, disp_s, disp_r, loc, nb_s, nb_r, sib_s, sib_r, wz_s, wz_r, ag_s, ag_r,
    dx_s, dx_r, dn_s, dn_r, ret_s, ret_r, rs_s, rs_r, zs_s, zs_r,
):
    di, ei = lax.axis_index("dp"), lax.axis_index("expert")
    y, c = di // 2, di % 2
    x, z = ei // NZ, ei % NZ
    h, zl = z // 4, z % 4
    sibling = {"dp": y * 2 + (1 - c), "expert": ei}
    above = {"dp": ((y + 1) % NY) * 2 + c, "expert": ei}
    below = {"dp": ((y + NY - 1) % NY) * 2 + c, "expert": ei}
    beside = {"dp": di, "expert": x * NZ + z + 1 - 2 * (z % 2)}

    def at_x(dx, rel):
        return ((x + dx) % NX) * NZ + (z if rel == 0 else NZ - 1 - z)

    def mirror(core):
        return {"dp": y * 2 + core, "expert": x * NZ + h * 4 + 3 - zl}

    far = [(0, 1), (1, 0), (3, 0), (2, 0), (1, 1), (3, 1), (2, 1)]

    def remote(src, dst, send, recv, where):
        return pltpu.make_async_remote_copy(
            src_ref=src, dst_ref=dst, send_sem=send, recv_sem=recv,
            device_id=where, device_id_type=MESH,
        )

    barrier = pltpu.get_barrier_semaphore()
    partners = [sibling, above, below, beside, mirror(0), mirror(1)]
    partners += [{"dp": di, "expert": at_x(dx, rel)} for dx, rel in far]
    for p in partners:
        pl.semaphore_signal(barrier, inc=1, device_id=p, device_id_type=MESH)

    half_hid = pl.ds(pl.multiple_of(c * HALF_HID, HALF_HID), HALF_HID)

    def own_block(b):
        cols = pl.ds(pl.multiple_of(b * BLK, BLK), BLK)
        return [
            pltpu.make_async_copy(
                w.at[half_hid, cols], wall.at[0, b, pl.ds(m * HALF_HID, HALF_HID)], own_s.at[b, m]
            )
            for m, w in enumerate((gp, up, dn))
        ]

    for k in range(NY):
        for w in own_block((y + k) % NY):
            w.start()

    route = routes[...]
    one_hot = pick(iota((16, TOK), 0) == route)
    earlier = pick(iota((TOK, TOK), 0) < iota((TOK, TOK), 1))
    rank = jnp.sum(dot(one_hot, earlier) * one_hot.astype(F32), axis=0, keepdims=True)
    rank = rank.astype(jnp.int32)
    low = rank < 16
    slots = iota((EXPERTS * 32, TOK), 0)
    main = jnp.where(low, route * 32 + rank, -1)
    place = jnp.concatenate(
        [pick(slots == main), pick(slots == jnp.where(low, main + 16, -1))], axis=1
    )
    slots = iota((EXPERTS * 16, TOK), 0)
    diagonal = iota((TOK, TOK), 0) == iota((TOK, TOK), 1)
    weight = jnp.sum(jnp.where(diagonal, gates[...], 0.0), axis=1, keepdims=True)
    rest = jnp.zeros((EXPERTS * 16, WIDE), F32)
    for b in range(4):
        cols = slice(b * WIDE, b * WIDE + WIDE)
        scaled = (cot[:, cols].astype(F32) * weight).astype(BF16)
        both = jnp.concatenate([tok[:, cols], scaled], axis=0)
        out = dot(place, both).astype(BF16)
        over = jnp.where(low, -1, route * 16 + 4 * b + rank - 16)
        over = jnp.concatenate(
            [pick(slots == over), pick(slots == jnp.where(low, -1, over + 2))], axis=1
        )
        rest = rest + dot(over, both)
        for e in range(EXPERTS):
            xd[e * MSG + b * 32:e * MSG + b * 32 + 32] = out[e * 32:e * 32 + 32]
    rest = rest.astype(BF16)
    for e in range(EXPERTS):
        xd[e * MSG + 128:e * MSG + MSG] = rest[e * 16:e * 16 + 16]

    for w in own_block(y):
        w.wait()
    pl.semaphore_wait(barrier, len(partners))
    wz = remote(wall.at[0, y], wall.at[1, y], wz_s, wz_r, mirror(c))
    wz.start()

    def msg(e):
        return pl.ds(pl.multiple_of(e * MSG, MSG), MSG)

    sends = []
    for i, (dx, rel) in enumerate(far):
        e = ((x + dx) % NX) * 2 + (h if rel == 0 else 1 - h)
        sends.append(
            remote(
                xd.at[msg(e)], rcv.at[c, msg(x * 2 + rel)],
                disp_s.at[i], disp_r.at[i], {"dp": di, "expert": at_x(dx, rel)},
            )
        )
        sends[-1].start()
    keep = pltpu.make_async_copy(xd.at[msg(x * 2 + h)], rcv.at[c, msg(x * 2)], loc)
    keep.start()

    def slot(i):
        dx, rel = (far + [(0, 0)])[i]
        return msg(((x - dx + NX) % NX) * 2 + rel)

    def to_beside(i):
        return remote(
            rcv.at[c, slot(i)], rcv.at[2 + c, slot(i)], nb_s.at[i], nb_r.at[i], beside
        )

    def from_beside(i):
        return remote(rcv.at[c, slot(i)], rcv.at[2 + c, slot(i)], nb_s.at[i], nb_r.at[i], beside)

    def to_sibling(n, i):
        ref = rcv.at[2 * n + c, slot(i)]
        return remote(ref, ref, sib_s.at[n, i], sib_r.at[n, i], sibling)

    def from_sibling(n, i):
        ref = rcv.at[2 * n + 1 - c, slot(i)]
        return remote(ref, ref, sib_s.at[n, i], sib_r.at[n, i], sibling)

    def ag(way, t):
        b = (y - t + NY) % NY if way == 0 else (y + t) % NY
        ref = wall.at[1, b]
        if t == 3:
            ref = wall.at[1, b, pl.ds(way * (WROWS // 2), WROWS // 2)]
        return remote(ref, ref, ag_s.at[way, t], ag_r.at[way, t], above if way == 0 else below)

    def ag_in(way, t):
        b = (y - 1 - t + NY) % NY if way == 0 else (y + 1 + t) % NY
        ref = wall.at[1, b]
        if t == 3:
            ref = wall.at[1, b, pl.ds(way * (WROWS // 2), WROWS // 2)]
        remote(ref, ref, ag_s.at[way, t], ag_r.at[way, t], above if way == 0 else below).wait_recv()

    def ag_step(t):
        for way in (0, 1):
            ag_in(way, t - 1)
            ag(way, t).start()

    def forward(i):
        if i < 7:
            sends[i].wait_recv()
        else:
            keep.wait()
        to_beside(i).start()
        to_sibling(0, i).start()

    def forward_beside(i):
        from_beside(i).wait_recv()
        to_sibling(1, i).start()

    row = iota((ROWS, 1), 0)
    source = jnp.zeros((ROWS, 1), jnp.int32)
    for m in range(1, EXPERTS):
        source = source + jnp.where(row >= MOST * m, 1, 0)
    row = row - MOST * source
    col = iota((ROWS, EXPERTS * 48), 1)

    def gather_rows(g, n):
        for i in ((0, 4, 5, 6) if g else (7, 1, 2, 3)):
            from_sibling(n, i).wait_recv()
        at = slice((2 * g + n) * ROWS, (2 * g + n) * ROWS + ROWS)
        messages = [(rcv, (2 * n + k // 4,), (2 * (k % 4) + g) * MSG) for k in range(EXPERTS)]
        for b in range(4):
            cols = slice(b * WIDE, b * WIDE + WIDE)
            sel_x = pick(col == jnp.where(row < 16, source * 32 + row, 240 + source * 16 + 4 * b + row))
            sel_d = pick(col == jnp.where(row < 16, source * 32 + 16 + row, 242 + source * 16 + 4 * b + row))
            rows = packed(messages, b * 32, 32)
            xs[at, cols] = dot(sel_x, rows).astype(BF16)
            ds[at, cols] = dot(sel_d, rows).astype(BF16)

    def group(g):
        return slice(g * 2 * ROWS, (g + 1) * 2 * ROWS)

    def activations(g, s):
        pre = jnp.zeros((GU, 2 * ROWS), F32)
        dh = jnp.zeros((HALF_HID, 2 * ROWS), F32)
        for b in range(NY):
            cols = slice(b * BLK, b * BLK + BLK)
            pre = pre + dot(wall[s, b, 0:GU, :], xs[group(g), cols], NT)
            dh = dh + dot(wall[s, b, GU:WROWS, :], ds[group(g), cols], NT)
        gate, u = pre[0:HALF_HID], pre[HALF_HID:GU]
        sig = 1.0 / (1.0 + jnp.exp(-gate))
        hid[g, s * HALF_HID:s * HALF_HID + HALF_HID] = (gate * sig * u).astype(BF16)
        dgu[g, s * GU:s * GU + HALF_HID] = (dh * u * sig * (1.0 + gate * (1.0 - sig))).astype(BF16)
        dgu[g, s * GU + HALF_HID:s * GU + GU] = (dh * gate * sig).astype(BF16)

    j, i_ = iota((EXPERTS * 16, ROWS), 0), iota((EXPERTS * 16, ROWS), 1)
    spread = pick(i_ == j + 2 * (j // 16))

    def dx_out(g, n):
        return remote(dxp.at[g, 2 * n + 1 - c], dxr.at[g, n], dx_s.at[g, n], dx_r.at[g, n], sibling)

    def input_grads(g):
        lasts = [jnp.zeros((EXPERTS * 16, BLK), F32) for _ in range(2)]
        for b in range(NY):
            cols = slice(b * BLK, b * BLK + BLK)
            rhs = jnp.concatenate([wall[s, b, 0:GU, :] for s in (0, 1)], axis=0)
            dx = dot(dgu[g], rhs, TN).astype(BF16)
            own = j % 16 - 2 * b
            spread_last = pick((i_ == MOST * (j // 16) + 16 + own) & (own >= 0) & (own < 2))
            for n in (0, 1):
                mine = dx[n * ROWS:n * ROWS + ROWS]
                out = dot(spread, mine).astype(BF16)
                lasts[n] = lasts[n] + dot(spread_last, mine)
                for k in range(EXPERTS):
                    at = (k % 4) * MSG + b * 16
                    dxp[g, 2 * n + k // 4, at:at + 16] = out[k * 16:k * 16 + 16]
        for n in (1, 0):
            last = lasts[n].astype(BF16)
            for k in range(EXPERTS):
                at = (k % 4) * MSG + 128
                dxp[g, 2 * n + k // 4, at:at + 16] = last[k * 16:k * 16 + 16]
            dx_out(g, n).start()

    def dx_beside(g):
        return remote(dxr.at[g, 1], dxn.at[g], dn_s.at[g], dn_r.at[g], beside)

    def sum_for_beside(g):
        dx_out(g, 1).wait_recv()
        dxr[g, 1] = (dxr[g, 1].astype(F32) + dxp[g, 2 + c].astype(F32)).astype(BF16)
        dx_beside(g).start()

    backs = []
    back_own = pltpu.make_async_copy(dxr.at[0, 0, msg(x)], ret.at[msg(x * 2 + h)], loc)

    def send_back(g):
        dx_out(g, 0).wait_recv()
        dx_beside(g).wait_recv()
        dxr[g, 0] = (dxr[g, 0].astype(F32) + dxp[g, c].astype(F32) + dxn[g].astype(F32)).astype(BF16)
        for i, (dx, rel) in enumerate(far):
            if rel == g:
                backs.append(
                    remote(
                        dxr.at[g, 0, msg((x + dx) % NX)], ret.at[msg(x * 2 + h)],
                        ret_s.at[i], ret_r.at[i], {"dp": di, "expert": at_x(dx, rel)},
                    )
                )
                backs[-1].start()
        if g == 0:
            back_own.start()

    def rs(way, t, s):
        if t == 0:
            half = pl.ds(way * (WROWS // 2), WROWS // 2)
            src, dst = gr.at[s, (y + 4) % NY, half], rb.at[way, 0, s, half]
        else:
            src, dst = rb.at[way, t - 1, s], rb.at[way, t, s]
        return remote(
            src, dst, rs_s.at[way, t, s], rs_r.at[way, t, s], above if way == 0 else below
        )

    def weight_grads(s, b):
        cols = pl.ds(pl.multiple_of(b * BLK, BLK), BLK)
        gu, dn_ = jnp.zeros((GU, BLK), F32), jnp.zeros((HALF_HID, BLK), F32)
        for g in (0, 1):
            gu = gu + dot(dgu[g, s * GU:s * GU + GU], xs[group(g), cols])
            dn_ = dn_ + dot(hid[g, s * HALF_HID:s * HALF_HID + HALF_HID], ds[group(g), cols])
        gr[s, b, 0:GU, :] = gu.astype(BF16)
        gr[s, b, GU:WROWS, :] = dn_.astype(BF16)

    def grads_at(distance):
        for s in (1, 0):
            for b in sorted({distance, (NY - distance) % NY}):
                weight_grads(s, (y + b) % NY)

    def rs_add(way, t, s):
        rs(way, t, s).wait_recv()
        b = (y + 3 - t) % NY if way == 0 else (y - 3 + t + NY) % NY
        if t == 0:
            lo, hi = way * (WROWS // 2), (1 - way) * (WROWS // 2)
            a, o = pl.ds(lo, WROWS // 2), pl.ds(hi, WROWS // 2)
            rb[way, 0, s, a, :] = (rb[way, 0, s, a, :].astype(F32) + gr[s, b, a, :].astype(F32)).astype(BF16)
            rb[way, 0, s, o, :] = gr[s, b, o, :]
        else:
            rb[way, t, s] = (rb[way, t, s].astype(F32) + gr[s, b].astype(F32)).astype(BF16)

    def rs_step(t):
        for s in (1, 0):
            for way in (0, 1):
                rs_add(way, t, s)
                rs(way, t + 1, s).start()

    forward(7)
    wz.wait_recv()
    for way in (0, 1):
        ag(way, 0).start()
    for i in (1, 2, 0, 3):
        forward(i)
    ag_step(1)
    for i in (7, 1, 2, 3):
        forward_beside(i)
    forward(4)
    ag_step(2)
    gather_rows(0, 0)
    forward(5)
    gather_rows(0, 1)
    ag_step(3)
    for k in range(1, NY):
        for w in own_block((y + k) % NY):
            w.wait()
    forward(6)
    forward_beside(0)
    activations(0, 0)
    forward_beside(4)
    for way in (0, 1):
        ag_in(way, 3)
    activations(0, 1)
    forward_beside(5)
    input_grads(0)
    forward_beside(6)
    gather_rows(1, 0)
    gather_rows(1, 1)
    activations(1, 1)
    activations(1, 0)
    for s in (1, 0):
        weight_grads(s, (y + 4) % NY)
        for way in (0, 1):
            rs(way, 0, s).start()
    sum_for_beside(0)
    input_grads(1)
    grads_at(3)
    sum_for_beside(1)
    rs_step(0)
    send_back(0)
    grads_at(2)
    rs_step(1)
    send_back(1)
    grads_at(1)
    rs_step(2)
    grads_at(0)

    finals = []
    for s in (1, 0):
        for way in (0, 1):
            rs(way, 3, s).wait_recv()
        total = gr[s, y].astype(F32) + rb[0, 3, s].astype(F32) + rb[1, 3, s].astype(F32)
        for core in (0, 1):
            tot[s, core] = total[:, core * 128:core * 128 + 128].astype(BF16)
        if s:
            for core in (0, 1):
                finals.append(
                    remote(tot.at[1, core], zb.at[1, c], zs_s.at[core], zs_r.at[1, c], mirror(core))
                )
                finals[-1].start()
        else:
            finals.append(remote(tot.at[0, 1 - c], zb.at[0, c], zs_s.at[2], zs_r.at[0, c], sibling))
            finals[-1].start()
            zb[0, c] = tot[0, c]

    back_own.wait()
    for b in backs:
        b.wait_recv()

    def column(row):
        held = jnp.sum(jnp.where(diagonal, row.astype(F32), 0.0), axis=1, keepdims=True)
        return held.astype(jnp.int32)

    route, rank = column(route), column(rank)
    cols_of = iota((TOK, EXPERTS * 32), 1)
    for b in range(NY):
        at = jnp.where(rank < 16, route * 16 + rank, 112 + route * 16 + 2 * b + rank)
        take = pick(cols_of == at)
        rows = packed([(ret, (), k * MSG) for k in range(EXPERTS)], b * 16, 16)
        gin[:, b * BLK:b * BLK + BLK] = dot(take, rows).astype(BF16)

    remote(tot.at[0, c], zb.at[0, 1 - c], zs_s.at[0], zs_r.at[0, 1 - c], sibling).wait_recv()
    for core in (0, 1):
        remote(tot.at[1, core], zb.at[1, core], zs_s.at[0], zs_r.at[1, core], sibling).wait_recv()
    for core in (0, 1):
        acc = zb[0, core].astype(F32) + zb[1, core].astype(F32)
        for m in range(3):
            grads[m, core * HALF_HID:(core + 1) * HALF_HID] = acc[m * HALF_HID:(m + 1) * HALF_HID]

    for w in [wz] + sends + finals + backs:
        w.wait_send()
    for g in (0, 1):
        dx_beside(g).wait_send()
        for n in (0, 1):
            dx_out(g, n).wait_send()
    for i in range(8):
        to_beside(i).wait_send()
        for n in (0, 1):
            to_sibling(n, i).wait_send()
    for way in (0, 1):
        for t in range(4):
            ag(way, t).wait_send()
            for s in (0, 1):
                rs(way, t, s).wait_send()


def body(tokens, cotangent, routes, expert_gates, gate_proj, up_proj, down_proj):
    vmem = pl.BlockSpec(memory_space=pltpu.VMEM)
    dma = pltpu.SemaphoreType.DMA
    anywhere = pl.BlockSpec(memory_space=pl.ANY)
    gin, grads = pl.pallas_call(
        kernel,
        out_shape=(
            jax.ShapeDtypeStruct((TOK, D), BF16),
            jax.ShapeDtypeStruct((3, GU, 128), F32),
        ),
        in_specs=[vmem] * 4 + [anywhere] * 3,
        out_specs=(vmem, vmem),
        scratch_shapes=[
            pltpu.VMEM((EXPERTS * MSG, WIDE), BF16),
            pltpu.VMEM((2, NY, WROWS, BLK), BF16),
            pltpu.VMEM((4, EXPERTS * MSG, WIDE), BF16),
            pltpu.VMEM((4 * ROWS, D), BF16),
            pltpu.VMEM((4 * ROWS, D), BF16),
            pltpu.VMEM((2, NY, WROWS, BLK), BF16),
            pltpu.VMEM((2, 4, 2, WROWS, BLK), BF16),
            pltpu.VMEM((2, 2, WROWS, 128), BF16),
            pltpu.VMEM((2, 2, WROWS, 128), BF16),
            pltpu.VMEM((2, 4, NX * MSG, BLK), BF16),
            pltpu.VMEM((2, 2, NX * MSG, BLK), BF16),
            pltpu.VMEM((2, NX * MSG, BLK), BF16),
            pltpu.VMEM((EXPERTS * MSG, BLK), BF16),
            pltpu.VMEM((2, 2 * GU, 2 * ROWS), BF16),
            pltpu.VMEM((2, 2 * HALF_HID, 2 * ROWS), BF16),
            dma((NY, 3)), dma((7,)), dma((7,)), dma, dma((8,)), dma((8,)), dma((2, 8)), dma((2, 8)),
            dma, dma, dma((2, 4)), dma((2, 4)), dma((2, 2)), dma((2, 2)), dma((2,)), dma((2,)),
            dma((7,)), dma((7,)), dma((2, 4, 2)), dma((2, 4, 2)), dma((3,)), dma((2, 2)),
        ],
        compiler_params=pltpu.CompilerParams(
            collective_id=0, has_side_effects=True, vmem_limit_bytes=56 * 2**20
        ),
    )(
        routes.reshape(1, TOK), expert_gates.reshape(1, TOK), tokens, cotangent,
        gate_proj.T, up_proj.T, down_proj,
    )
    return gin, grads[0].T, grads[1].T, grads[2]


def solution(mesh):
    in_specs = (
        P(("dp", "expert"), None),
        P(("dp", "expert"), None),
        P(("dp", "expert"), None),
        P(("dp", "expert"), None),
        P(None, "expert"),
        P(None, "expert"),
        P("expert", None),
    )
    out_specs = (P(("dp", "expert"), None), P("dp", "expert"), P("dp", "expert"), P("expert", "dp"))
    return jax.shard_map(body, mesh=mesh, in_specs=in_specs, out_specs=out_specs, check_vma=False)
```

```python
import jax
import jax.numpy as jnp
from jax import lax
from jax.experimental import pallas as pl
from jax.experimental.pallas import tpu as pltpu
from jax.sharding import PartitionSpec as P

MESH = pl.DeviceIdType.MESH
EXPERTS = 8
MOST = 18
TOK = 128
D = 2048
NX, NY, NZ = 4, 8, 8
HALF_HID = 96
WROWS = 3 * HALF_HID
GU = 2 * HALF_HID
BLK = D // NY
ROWS = EXPERTS * MOST
WIDE = 512
MSG = 144
F32 = jnp.float32
BF16 = jnp.bfloat16
NT = (((1,), (1,)), ((), ()))
TN = (((0,), (0,)), ((), ()))
NN = (((1,), (0,)), ((), ()))


def dot(a, b, dims=NN):
    return lax.dot_general(a, b, dims, preferred_element_type=F32)


def iota(shape, dim):
    return lax.broadcasted_iota(jnp.int32, shape, dim)


def pick(cond):
    return jnp.where(cond, 1.0, 0.0).astype(BF16)


def packed(messages, start, size):
    parts = [ref[(*lead, slice(at + start, at + start + size))] for ref, lead, at in messages]
    parts += [ref[(*lead, slice(at + 128, at + MSG))] for ref, lead, at in messages]
    return jnp.concatenate(parts, axis=0)


def kernel(
    routes, gates, tok, cot, gp, up, dn, gin, grads,
    xd, wall, rcv, xs, ds, gr, rb, tot, zb, dxp, dxr, dxn, ret, dgu, hid,
    own_s, disp_s, disp_r, loc, nb_s, nb_r, sib_s, sib_r, wz_s, wz_r, ag_s, ag_r,
    dx_s, dx_r, dn_s, dn_r, ret_s, ret_r, rs_s, rs_r, zs_s, zs_r,
):
    di, ei = lax.axis_index("dp"), lax.axis_index("expert")
    y, c = di // 2, di % 2
    x, z = ei // NZ, ei % NZ
    h, zl = z // 4, z % 4
    sibling = {"dp": y * 2 + (1 - c), "expert": ei}
    above = {"dp": ((y + 1) % NY) * 2 + c, "expert": ei}
    below = {"dp": ((y + NY - 1) % NY) * 2 + c, "expert": ei}
    beside = {"dp": di, "expert": x * NZ + z + 1 - 2 * (z % 2)}

    def at_x(dx, rel):
        return ((x + dx) % NX) * NZ + (z if rel == 0 else NZ - 1 - z)

    def mirror(core):
        return {"dp": y * 2 + core, "expert": x * NZ + h * 4 + 3 - zl}

    far = [(0, 1), (1, 0), (3, 0), (2, 0), (1, 1), (3, 1), (2, 1)]

    def remote(src, dst, send, recv, where):
        return pltpu.make_async_remote_copy(
            src_ref=src, dst_ref=dst, send_sem=send, recv_sem=recv,
            device_id=where, device_id_type=MESH,
        )

    barrier = pltpu.get_barrier_semaphore()
    partners = [sibling, above, below, beside, mirror(0), mirror(1)]
    partners += [{"dp": di, "expert": at_x(dx, rel)} for dx, rel in far]
    for p in partners:
        pl.semaphore_signal(barrier, inc=1, device_id=p, device_id_type=MESH)

    half_hid = pl.ds(pl.multiple_of(c * HALF_HID, HALF_HID), HALF_HID)

    def own_block(b):
        cols = pl.ds(pl.multiple_of(b * BLK, BLK), BLK)
        return [
            pltpu.make_async_copy(
                w.at[half_hid, cols], wall.at[0, b, pl.ds(m * HALF_HID, HALF_HID)], own_s.at[b, m]
            )
            for m, w in enumerate((gp, up, dn))
        ]

    for k in range(NY):
        for w in own_block((y + k) % NY):
            w.start()

    route = routes[...]
    one_hot = pick(iota((16, TOK), 0) == route)
    earlier = pick(iota((TOK, TOK), 0) < iota((TOK, TOK), 1))
    rank = jnp.sum(dot(one_hot, earlier) * one_hot.astype(F32), axis=0, keepdims=True)
    rank = rank.astype(jnp.int32)
    low = rank < 16
    slots = iota((EXPERTS * 32, TOK), 0)
    main = jnp.where(low, route * 32 + rank, -1)
    place = jnp.concatenate(
        [pick(slots == main), pick(slots == jnp.where(low, main + 16, -1))], axis=1
    )
    slots = iota((EXPERTS * 16, TOK), 0)
    diagonal = iota((TOK, TOK), 0) == iota((TOK, TOK), 1)
    weight = jnp.sum(jnp.where(diagonal, gates[...], 0.0), axis=1, keepdims=True)
    rest = jnp.zeros((EXPERTS * 16, WIDE), F32)
    for b in range(4):
        cols = slice(b * WIDE, b * WIDE + WIDE)
        scaled = (cot[:, cols].astype(F32) * weight).astype(BF16)
        both = jnp.concatenate([tok[:, cols], scaled], axis=0)
        out = dot(place, both).astype(BF16)
        over = jnp.where(low, -1, route * 16 + 4 * b + rank - 16)
        over = jnp.concatenate(
            [pick(slots == over), pick(slots == jnp.where(low, -1, over + 2))], axis=1
        )
        rest = rest + dot(over, both)
        for e in range(EXPERTS):
            xd[e * MSG + b * 32:e * MSG + b * 32 + 32] = out[e * 32:e * 32 + 32]
    rest = rest.astype(BF16)
    for e in range(EXPERTS):
        xd[e * MSG + 128:e * MSG + MSG] = rest[e * 16:e * 16 + 16]

    for w in own_block(y):
        w.wait()
    pl.semaphore_wait(barrier, len(partners))
    wz = remote(wall.at[0, y], wall.at[1, y], wz_s, wz_r, mirror(c))
    wz.start()

    def msg(e):
        return pl.ds(pl.multiple_of(e * MSG, MSG), MSG)

    sends = []
    for i, (dx, rel) in enumerate(far):
        e = ((x + dx) % NX) * 2 + (h if rel == 0 else 1 - h)
        sends.append(
            remote(
                xd.at[msg(e)], rcv.at[c, msg(x * 2 + rel)],
                disp_s.at[i], disp_r.at[i], {"dp": di, "expert": at_x(dx, rel)},
            )
        )
        sends[-1].start()
    keep = pltpu.make_async_copy(xd.at[msg(x * 2 + h)], rcv.at[c, msg(x * 2)], loc)
    keep.start()

    def slot(i):
        dx, rel = (far + [(0, 0)])[i]
        return msg(((x - dx + NX) % NX) * 2 + rel)

    def to_beside(i):
        return remote(
            rcv.at[c, slot(i)], rcv.at[2 + c, slot(i)], nb_s.at[i], nb_r.at[i], beside
        )

    def from_beside(i):
        return remote(rcv.at[c, slot(i)], rcv.at[2 + c, slot(i)], nb_s.at[i], nb_r.at[i], beside)

    def to_sibling(n, i):
        ref = rcv.at[2 * n + c, slot(i)]
        return remote(ref, ref, sib_s.at[n, i], sib_r.at[n, i], sibling)

    def from_sibling(n, i):
        ref = rcv.at[2 * n + 1 - c, slot(i)]
        return remote(ref, ref, sib_s.at[n, i], sib_r.at[n, i], sibling)

    def ag(way, t):
        b = (y - t + NY) % NY if way == 0 else (y + t) % NY
        ref = wall.at[1, b]
        if t == 3:
            ref = wall.at[1, b, pl.ds(way * (WROWS // 2), WROWS // 2)]
        return remote(ref, ref, ag_s.at[way, t], ag_r.at[way, t], above if way == 0 else below)

    def ag_in(way, t):
        b = (y - 1 - t + NY) % NY if way == 0 else (y + 1 + t) % NY
        ref = wall.at[1, b]
        if t == 3:
            ref = wall.at[1, b, pl.ds(way * (WROWS // 2), WROWS // 2)]
        remote(ref, ref, ag_s.at[way, t], ag_r.at[way, t], above if way == 0 else below).wait_recv()

    def ag_step(t):
        for way in (0, 1):
            ag_in(way, t - 1)
            ag(way, t).start()

    def forward(i):
        if i < 7:
            sends[i].wait_recv()
        else:
            keep.wait()
        to_beside(i).start()
        to_sibling(0, i).start()

    def forward_beside(i):
        from_beside(i).wait_recv()
        to_sibling(1, i).start()

    row = iota((ROWS, 1), 0)
    source = jnp.zeros((ROWS, 1), jnp.int32)
    for m in range(1, EXPERTS):
        source = source + jnp.where(row >= MOST * m, 1, 0)
    row = row - MOST * source
    col = iota((ROWS, EXPERTS * 48), 1)

    def gather_rows(g, n):
        for i in ((0, 4, 5, 6) if g else (7, 1, 2, 3)):
            from_sibling(n, i).wait_recv()
        at = slice((2 * g + n) * ROWS, (2 * g + n) * ROWS + ROWS)
        messages = [(rcv, (2 * n + k // 4,), (2 * (k % 4) + g) * MSG) for k in range(EXPERTS)]
        for b in range(4):
            cols = slice(b * WIDE, b * WIDE + WIDE)
            sel_x = pick(col == jnp.where(row < 16, source * 32 + row, 240 + source * 16 + 4 * b + row))
            sel_d = pick(col == jnp.where(row < 16, source * 32 + 16 + row, 242 + source * 16 + 4 * b + row))
            rows = packed(messages, b * 32, 32)
            xs[at, cols] = dot(sel_x, rows).astype(BF16)
            ds[at, cols] = dot(sel_d, rows).astype(BF16)

    def part(p):
        return slice(p * ROWS, p * ROWS + ROWS)

    def activations(p, s):
        pre = jnp.zeros((GU, ROWS), F32)
        dh = jnp.zeros((HALF_HID, ROWS), F32)
        for b in range(NY):
            cols = slice(b * BLK, b * BLK + BLK)
            pre = pre + dot(wall[s, b, 0:GU, :], xs[part(p), cols], NT)
            dh = dh + dot(wall[s, b, GU:WROWS, :], ds[part(p), cols], NT)
        gate, u = pre[0:HALF_HID], pre[HALF_HID:GU]
        sig = 1.0 / (1.0 + jnp.exp(-gate))
        hid[p, s * HALF_HID:s * HALF_HID + HALF_HID] = (gate * sig * u).astype(BF16)
        dgu[p, s * GU:s * GU + HALF_HID] = (dh * u * sig * (1.0 + gate * (1.0 - sig))).astype(BF16)
        dgu[p, s * GU + HALF_HID:s * GU + GU] = (dh * gate * sig).astype(BF16)

    j, i_ = iota((EXPERTS * 16, ROWS), 0), iota((EXPERTS * 16, ROWS), 1)
    spread = pick(i_ == j + 2 * (j // 16))

    def dx_out(g, n):
        return remote(dxp.at[g, 2 * n + 1 - c], dxr.at[g, n], dx_s.at[g, n], dx_r.at[g, n], sibling)

    def input_grads(g, n):
        last = jnp.zeros((EXPERTS * 16, BLK), F32)
        for b in range(NY):
            cols = slice(b * BLK, b * BLK + BLK)
            rhs = jnp.concatenate([wall[s, b, 0:GU, :] for s in (0, 1)], axis=0)
            dx = dot(dgu[2 * g + n], rhs, TN).astype(BF16)
            own = j % 16 - 2 * b
            spread_last = pick((i_ == MOST * (j // 16) + 16 + own) & (own >= 0) & (own < 2))
            out = dot(spread, dx).astype(BF16)
            last = last + dot(spread_last, dx)
            for k in range(EXPERTS):
                at = (k % 4) * MSG + b * 16
                dxp[g, 2 * n + k // 4, at:at + 16] = out[k * 16:k * 16 + 16]
        last = last.astype(BF16)
        for k in range(EXPERTS):
            at = (k % 4) * MSG + 128
            dxp[g, 2 * n + k // 4, at:at + 16] = last[k * 16:k * 16 + 16]
        dx_out(g, n).start()

    def dx_beside(g, dx):
        at = msg((x + dx) % NX)
        return remote(dxr.at[g, 1, at], dxn.at[g, at], dn_s.at[g, dx], dn_r.at[g, dx], beside)

    def sum_for_beside(g):
        dx_out(g, 1).wait_recv()
        for dx in (0, 1, 3, 2):
            at = msg((x + dx) % NX)
            dxr[g, 1, at] = (dxr[g, 1, at].astype(F32) + dxp[g, 2 + c, at].astype(F32)).astype(BF16)
            dx_beside(g, dx).start()

    backs = []
    back_own = pltpu.make_async_copy(dxr.at[0, 0, msg(x)], ret.at[msg(x * 2 + h)], loc)

    def send_back(g, dx):
        at = msg((x + dx) % NX)
        dx_beside(g, dx).wait_recv()
        total = dxr[g, 0, at].astype(F32) + dxp[g, c, at].astype(F32) + dxn[g, at].astype(F32)
        dxr[g, 0, at] = total.astype(BF16)
        if (dx, g) == (0, 0):
            back_own.start()
            return
        i = far.index((dx, g))
        backs.append(
            remote(
                dxr.at[g, 0, at], ret.at[msg(x * 2 + h)],
                ret_s.at[i], ret_r.at[i], {"dp": di, "expert": at_x(dx, g)},
            )
        )
        backs[-1].start()

    def rs(way, t, s):
        if t == 0:
            half = pl.ds(way * (WROWS // 2), WROWS // 2)
            src, dst = gr.at[s, (y + 4) % NY, half], rb.at[way, 0, s, half]
        else:
            src, dst = rb.at[way, t - 1, s], rb.at[way, t, s]
        return remote(
            src, dst, rs_s.at[way, t, s], rs_r.at[way, t, s], above if way == 0 else below
        )

    def weight_grads(s, b):
        cols = pl.ds(pl.multiple_of(b * BLK, BLK), BLK)
        gu, dn_ = jnp.zeros((GU, BLK), F32), jnp.zeros((HALF_HID, BLK), F32)
        for p in range(4):
            gu = gu + dot(dgu[p, s * GU:s * GU + GU], xs[part(p), cols])
            dn_ = dn_ + dot(hid[p, s * HALF_HID:s * HALF_HID + HALF_HID], ds[part(p), cols])
        gr[s, b, 0:GU, :] = gu.astype(BF16)
        gr[s, b, GU:WROWS, :] = dn_.astype(BF16)

    def grads_at(distance):
        for s in (1, 0):
            for b in sorted({distance, (NY - distance) % NY}):
                weight_grads(s, (y + b) % NY)

    def rs_add(way, t, s):
        rs(way, t, s).wait_recv()
        b = (y + 3 - t) % NY if way == 0 else (y - 3 + t + NY) % NY
        if t == 0:
            lo, hi = way * (WROWS // 2), (1 - way) * (WROWS // 2)
            a, o = pl.ds(lo, WROWS // 2), pl.ds(hi, WROWS // 2)
            rb[way, 0, s, a, :] = (rb[way, 0, s, a, :].astype(F32) + gr[s, b, a, :].astype(F32)).astype(BF16)
            rb[way, 0, s, o, :] = gr[s, b, o, :]
        else:
            rb[way, t, s] = (rb[way, t, s].astype(F32) + gr[s, b].astype(F32)).astype(BF16)

    def rs_step(t):
        for s in (1, 0):
            for way in (0, 1):
                rs_add(way, t, s)
                rs(way, t + 1, s).start()

    forward(7)
    wz.wait_recv()
    for way in (0, 1):
        ag(way, 0).start()
    for i in (1, 2, 3, 0):
        forward(i)
    ag_step(1)
    forward(4)
    ag_step(2)
    forward(5)
    ag_step(3)
    forward(6)
    for i in (7, 1, 2, 3):
        forward_beside(i)
    for k in range(1, NY):
        for w in own_block((y + k) % NY):
            w.wait()
    for n in (0, 1):
        gather_rows(0, n)
        activations(n, 0)
    for way in (0, 1):
        ag_in(way, 3)
    for n in (1, 0):
        activations(n, 1)
        input_grads(0, n)
    gather_rows(1, 0)
    activations(2, 0)
    activations(2, 1)
    for i in (0, 4, 5, 6):
        forward_beside(i)
    sum_for_beside(0)
    gather_rows(1, 1)
    for s in (1, 0):
        activations(3, s)
        weight_grads(s, (y + 4) % NY)
        for way in (0, 1):
            rs(way, 0, s).start()
    input_grads(1, 1)
    sum_for_beside(1)
    input_grads(1, 0)
    grads_at(3)
    dx_out(0, 0).wait_recv()
    rs_step(0)
    for dx in (0, 1, 3, 2):
        send_back(0, dx)
    dx_out(1, 0).wait_recv()
    for dx in (0, 1):
        send_back(1, dx)
    grads_at(2)
    for dx in (3, 2):
        send_back(1, dx)
    rs_step(1)
    grads_at(1)
    rs_step(2)
    grads_at(0)

    finals = []
    for s in (1, 0):
        for way in (0, 1):
            rs(way, 3, s).wait_recv()
        total = gr[s, y].astype(F32) + rb[0, 3, s].astype(F32) + rb[1, 3, s].astype(F32)
        for core in (0, 1):
            tot[s, core] = total[:, core * 128:core * 128 + 128].astype(BF16)
        if s:
            for core in (0, 1):
                finals.append(
                    remote(tot.at[1, core], zb.at[1, c], zs_s.at[core], zs_r.at[1, c], mirror(core))
                )
                finals[-1].start()
        else:
            finals.append(remote(tot.at[0, 1 - c], zb.at[0, c], zs_s.at[2], zs_r.at[0, c], sibling))
            finals[-1].start()
            zb[0, c] = tot[0, c]

    back_own.wait()
    for b in backs:
        b.wait_recv()

    def column(row):
        held = jnp.sum(jnp.where(diagonal, row.astype(F32), 0.0), axis=1, keepdims=True)
        return held.astype(jnp.int32)

    route, rank = column(route), column(rank)
    cols_of = iota((TOK, EXPERTS * 32), 1)
    for b in range(NY):
        at = jnp.where(rank < 16, route * 16 + rank, 112 + route * 16 + 2 * b + rank)
        take = pick(cols_of == at)
        rows = packed([(ret, (), k * MSG) for k in range(EXPERTS)], b * 16, 16)
        gin[:, b * BLK:b * BLK + BLK] = dot(take, rows).astype(BF16)

    remote(tot.at[0, c], zb.at[0, 1 - c], zs_s.at[0], zs_r.at[0, 1 - c], sibling).wait_recv()
    for core in (0, 1):
        remote(tot.at[1, core], zb.at[1, core], zs_s.at[0], zs_r.at[1, core], sibling).wait_recv()
    for core in (0, 1):
        acc = zb[0, core].astype(F32) + zb[1, core].astype(F32)
        for m in range(3):
            grads[m, core * HALF_HID:(core + 1) * HALF_HID] = acc[m * HALF_HID:(m + 1) * HALF_HID]

    for w in [wz] + sends + finals + backs:
        w.wait_send()
    for g in (0, 1):
        for dx in range(NX):
            dx_beside(g, dx).wait_send()
        for n in (0, 1):
            dx_out(g, n).wait_send()
    for i in range(8):
        to_beside(i).wait_send()
        for n in (0, 1):
            to_sibling(n, i).wait_send()
    for way in (0, 1):
        for t in range(4):
            ag(way, t).wait_send()
            for s in (0, 1):
                rs(way, t, s).wait_send()


def body(tokens, cotangent, routes, expert_gates, gate_proj, up_proj, down_proj):
    vmem = pl.BlockSpec(memory_space=pltpu.VMEM)
    dma = pltpu.SemaphoreType.DMA
    anywhere = pl.BlockSpec(memory_space=pl.ANY)
    gin, grads = pl.pallas_call(
        kernel,
        out_shape=(
            jax.ShapeDtypeStruct((TOK, D), BF16),
            jax.ShapeDtypeStruct((3, GU, 128), F32),
        ),
        in_specs=[vmem] * 4 + [anywhere] * 3,
        out_specs=(vmem, vmem),
        scratch_shapes=[
            pltpu.VMEM((EXPERTS * MSG, WIDE), BF16),
            pltpu.VMEM((2, NY, WROWS, BLK), BF16),
            pltpu.VMEM((4, EXPERTS * MSG, WIDE), BF16),
            pltpu.VMEM((4 * ROWS, D), BF16),
            pltpu.VMEM((4 * ROWS, D), BF16),
            pltpu.VMEM((2, NY, WROWS, BLK), BF16),
            pltpu.VMEM((2, 4, 2, WROWS, BLK), BF16),
            pltpu.VMEM((2, 2, WROWS, 128), BF16),
            pltpu.VMEM((2, 2, WROWS, 128), BF16),
            pltpu.VMEM((2, 4, NX * MSG, BLK), BF16),
            pltpu.VMEM((2, 2, NX * MSG, BLK), BF16),
            pltpu.VMEM((2, NX * MSG, BLK), BF16),
            pltpu.VMEM((EXPERTS * MSG, BLK), BF16),
            pltpu.VMEM((4, 2 * GU, ROWS), BF16),
            pltpu.VMEM((4, 2 * HALF_HID, ROWS), BF16),
            dma((NY, 3)), dma((7,)), dma((7,)), dma, dma((8,)), dma((8,)), dma((2, 8)), dma((2, 8)),
            dma, dma, dma((2, 4)), dma((2, 4)), dma((2, 2)), dma((2, 2)), dma((2, NX)), dma((2, NX)),
            dma((7,)), dma((7,)), dma((2, 4, 2)), dma((2, 4, 2)), dma((3,)), dma((2, 2)),
        ],
        compiler_params=pltpu.CompilerParams(
            collective_id=0, has_side_effects=True, vmem_limit_bytes=56 * 2**20
        ),
    )(
        routes.reshape(1, TOK), expert_gates.reshape(1, TOK), tokens, cotangent,
        gate_proj.T, up_proj.T, down_proj,
    )
    return gin, grads[0].T, grads[1].T, grads[2]


def solution(mesh):
    in_specs = (
        P(("dp", "expert"), None),
        P(("dp", "expert"), None),
        P(("dp", "expert"), None),
        P(("dp", "expert"), None),
        P(None, "expert"),
        P(None, "expert"),
        P("expert", None),
    )
    out_specs = (P(("dp", "expert"), None), P("dp", "expert"), P("dp", "expert"), P("expert", "dp"))
    return jax.shard_map(body, mesh=mesh, in_specs=in_specs, out_specs=out_specs, check_vma=False)
```

```python
import jax
import jax.numpy as jnp
from jax import lax
from jax.experimental import pallas as pl
from jax.experimental.pallas import tpu as pltpu
from jax.sharding import PartitionSpec as P

MESH = pl.DeviceIdType.MESH
EXPERTS = 8
MOST = 18
TOK = 128
D = 2048
NX, NY, NZ = 4, 8, 8
HALF_HID = 96
WROWS = 3 * HALF_HID
GU = 2 * HALF_HID
BLK = D // NY
ROWS = EXPERTS * MOST
WIDE = 512
MSG = 144
F32 = jnp.float32
BF16 = jnp.bfloat16
NT = (((1,), (1,)), ((), ()))
TN = (((0,), (0,)), ((), ()))
NN = (((1,), (0,)), ((), ()))


def dot(a, b, dims=NN):
    return lax.dot_general(a, b, dims, preferred_element_type=F32)


def iota(shape, dim):
    return lax.broadcasted_iota(jnp.int32, shape, dim)


def pick(cond):
    return jnp.where(cond, 1.0, 0.0).astype(BF16)


def packed(messages, start, size):
    parts = [ref[(*lead, slice(at + start, at + start + size))] for ref, lead, at in messages]
    parts += [ref[(*lead, slice(at + 128, at + MSG))] for ref, lead, at in messages]
    return jnp.concatenate(parts, axis=0)


def kernel(
    routes, gates, tok_in, cot_in, gp, up, dn, gin_out, grads,
    xd, wall, rcv, xs, ds, gr, rb, tot, zb, dxp, dxr, dxn, ret, dgu, hid, tok, cot, gin,
    io_s, own_s, disp_s, disp_r, loc, nb_s, nb_r, sib_s, sib_r, wz_s, wz_r, ag_s, ag_r,
    dx_s, dx_r, dn_s, dn_r, ret_s, ret_r, rs_s, rs_r, zs_s, zs_r,
):
    loads = [
        pltpu.make_async_copy(src, dst, io_s.at[k])
        for k, (src, dst) in enumerate(((tok_in, tok), (cot_in, cot)))
    ]
    for w in loads:
        w.start()
    di, ei = lax.axis_index("dp"), lax.axis_index("expert")
    y, c = di // 2, di % 2
    x, z = ei // NZ, ei % NZ
    h, zl = z // 4, z % 4
    sibling = {"dp": y * 2 + (1 - c), "expert": ei}
    above = {"dp": ((y + 1) % NY) * 2 + c, "expert": ei}
    below = {"dp": ((y + NY - 1) % NY) * 2 + c, "expert": ei}
    beside = {"dp": di, "expert": x * NZ + z + 1 - 2 * (z % 2)}

    def at_x(dx, rel):
        return ((x + dx) % NX) * NZ + (z if rel == 0 else NZ - 1 - z)

    def mirror(core):
        return {"dp": y * 2 + core, "expert": x * NZ + h * 4 + 3 - zl}

    far = [(0, 1), (1, 0), (3, 0), (2, 0), (1, 1), (3, 1), (2, 1)]

    def remote(src, dst, send, recv, where):
        return pltpu.make_async_remote_copy(
            src_ref=src, dst_ref=dst, send_sem=send, recv_sem=recv,
            device_id=where, device_id_type=MESH,
        )

    barrier = pltpu.get_barrier_semaphore()
    partners = [sibling, above, below, beside, mirror(0), mirror(1)]
    partners += [{"dp": di, "expert": at_x(dx, rel)} for dx, rel in far]
    for p in partners:
        pl.semaphore_signal(barrier, inc=1, device_id=p, device_id_type=MESH)

    half_hid = pl.ds(pl.multiple_of(c * HALF_HID, HALF_HID), HALF_HID)

    def own_block(b):
        cols = pl.ds(pl.multiple_of(b * BLK, BLK), BLK)
        return [
            pltpu.make_async_copy(
                w.at[half_hid, cols], wall.at[0, b, pl.ds(m * HALF_HID, HALF_HID)], own_s.at[b, m]
            )
            for m, w in enumerate((gp, up, dn))
        ]

    for w in own_block(y):
        w.start()

    route = routes[...]
    one_hot = pick(iota((16, TOK), 0) == route)
    earlier = pick(iota((TOK, TOK), 0) < iota((TOK, TOK), 1))
    rank = jnp.sum(dot(one_hot, earlier) * one_hot.astype(F32), axis=0, keepdims=True)
    rank = rank.astype(jnp.int32)
    low = rank < 16
    slots = iota((EXPERTS * 32, TOK), 0)
    main = jnp.where(low, route * 32 + rank, -1)
    place = jnp.concatenate(
        [pick(slots == main), pick(slots == jnp.where(low, main + 16, -1))], axis=1
    )
    slots = iota((EXPERTS * 16, TOK), 0)
    diagonal = iota((TOK, TOK), 0) == iota((TOK, TOK), 1)
    weight = jnp.sum(jnp.where(diagonal, gates[...], 0.0), axis=1, keepdims=True)
    rest = jnp.zeros((EXPERTS * 16, WIDE), F32)
    for w in loads:
        w.wait()
    for b in range(4):
        cols = slice(b * WIDE, b * WIDE + WIDE)
        scaled = (cot[:, cols].astype(F32) * weight).astype(BF16)
        both = jnp.concatenate([tok[:, cols], scaled], axis=0)
        out = dot(place, both).astype(BF16)
        over = jnp.where(low, -1, route * 16 + 4 * b + rank - 16)
        over = jnp.concatenate(
            [pick(slots == over), pick(slots == jnp.where(low, -1, over + 2))], axis=1
        )
        rest = rest + dot(over, both)
        for e in range(EXPERTS):
            xd[e * MSG + b * 32:e * MSG + b * 32 + 32] = out[e * 32:e * 32 + 32]
    rest = rest.astype(BF16)
    for e in range(EXPERTS):
        xd[e * MSG + 128:e * MSG + MSG] = rest[e * 16:e * 16 + 16]

    for w in own_block(y):
        w.wait()
    pl.semaphore_wait(barrier, len(partners))
    wz = remote(wall.at[0, y], wall.at[1, y], wz_s, wz_r, mirror(c))
    wz.start()

    def msg(e):
        return pl.ds(pl.multiple_of(e * MSG, MSG), MSG)

    sends = []
    for i, (dx, rel) in enumerate(far):
        e = ((x + dx) % NX) * 2 + (h if rel == 0 else 1 - h)
        sends.append(
            remote(
                xd.at[msg(e)], rcv.at[c, msg(x * 2 + rel)],
                disp_s.at[i], disp_r.at[i], {"dp": di, "expert": at_x(dx, rel)},
            )
        )
        sends[-1].start()
    keep = pltpu.make_async_copy(xd.at[msg(x * 2 + h)], rcv.at[c, msg(x * 2)], loc)
    keep.start()
    for k in range(1, NY):
        for w in own_block((y + k) % NY):
            w.start()

    def slot(i):
        dx, rel = (far + [(0, 0)])[i]
        return msg(((x - dx + NX) % NX) * 2 + rel)

    def to_beside(i):
        return remote(
            rcv.at[c, slot(i)], rcv.at[2 + c, slot(i)], nb_s.at[i], nb_r.at[i], beside
        )

    def from_beside(i):
        return remote(rcv.at[c, slot(i)], rcv.at[2 + c, slot(i)], nb_s.at[i], nb_r.at[i], beside)

    def to_sibling(n, i):
        ref = rcv.at[2 * n + c, slot(i)]
        return remote(ref, ref, sib_s.at[n, i], sib_r.at[n, i], sibling)

    def from_sibling(n, i):
        ref = rcv.at[2 * n + 1 - c, slot(i)]
        return remote(ref, ref, sib_s.at[n, i], sib_r.at[n, i], sibling)

    def ag(way, t):
        b = (y - t + NY) % NY if way == 0 else (y + t) % NY
        ref = wall.at[1, b]
        if t == 3:
            ref = wall.at[1, b, pl.ds(way * (WROWS // 2), WROWS // 2)]
        return remote(ref, ref, ag_s.at[way, t], ag_r.at[way, t], above if way == 0 else below)

    def ag_in(way, t):
        b = (y - 1 - t + NY) % NY if way == 0 else (y + 1 + t) % NY
        ref = wall.at[1, b]
        if t == 3:
            ref = wall.at[1, b, pl.ds(way * (WROWS // 2), WROWS // 2)]
        remote(ref, ref, ag_s.at[way, t], ag_r.at[way, t], above if way == 0 else below).wait_recv()

    def ag_step(t):
        for way in (0, 1):
            ag_in(way, t - 1)
            ag(way, t).start()

    def forward(i):
        if i < 7:
            sends[i].wait_recv()
        else:
            keep.wait()
        to_beside(i).start()
        to_sibling(0, i).start()

    def forward_beside(i):
        from_beside(i).wait_recv()
        to_sibling(1, i).start()

    row = iota((ROWS, 1), 0)
    source = jnp.zeros((ROWS, 1), jnp.int32)
    for m in range(1, EXPERTS):
        source = source + jnp.where(row >= MOST * m, 1, 0)
    row = row - MOST * source
    col = iota((ROWS, EXPERTS * 48), 1)

    def gather_rows(g, n):
        for i in ((0, 4, 5, 6) if g else (7, 1, 2, 3)):
            from_sibling(n, i).wait_recv()
        at = slice((2 * g + n) * ROWS, (2 * g + n) * ROWS + ROWS)
        messages = [(rcv, (2 * n + k // 4,), (2 * (k % 4) + g) * MSG) for k in range(EXPERTS)]
        for b in range(4):
            cols = slice(b * WIDE, b * WIDE + WIDE)
            sel_x = pick(col == jnp.where(row < 16, source * 32 + row, 240 + source * 16 + 4 * b + row))
            sel_d = pick(col == jnp.where(row < 16, source * 32 + 16 + row, 242 + source * 16 + 4 * b + row))
            rows = packed(messages, b * 32, 32)
            xs[at, cols] = dot(sel_x, rows).astype(BF16)
            ds[at, cols] = dot(sel_d, rows).astype(BF16)

    def part(p):
        return slice(p * ROWS, p * ROWS + ROWS)

    def activations(p, s):
        pre = jnp.zeros((GU, ROWS), F32)
        dh = jnp.zeros((HALF_HID, ROWS), F32)
        for b in range(NY):
            cols = slice(b * BLK, b * BLK + BLK)
            pre = pre + dot(wall[s, b, 0:GU, :], xs[part(p), cols], NT)
            dh = dh + dot(wall[s, b, GU:WROWS, :], ds[part(p), cols], NT)
        gate, u = pre[0:HALF_HID], pre[HALF_HID:GU]
        sig = 1.0 / (1.0 + jnp.exp(-gate))
        hid[p, s * HALF_HID:s * HALF_HID + HALF_HID] = (gate * sig * u).astype(BF16)
        dgu[p, s * GU:s * GU + HALF_HID] = (dh * u * sig * (1.0 + gate * (1.0 - sig))).astype(BF16)
        dgu[p, s * GU + HALF_HID:s * GU + GU] = (dh * gate * sig).astype(BF16)

    j, i_ = iota((EXPERTS * 16, ROWS), 0), iota((EXPERTS * 16, ROWS), 1)
    spread = pick(i_ == j + 2 * (j // 16))

    def dx_out(g, n):
        return remote(dxp.at[g, 2 * n + 1 - c], dxr.at[g, n], dx_s.at[g, n], dx_r.at[g, n], sibling)

    def input_grads(g, n):
        last = jnp.zeros((EXPERTS * 16, BLK), F32)
        for b in range(NY):
            cols = slice(b * BLK, b * BLK + BLK)
            rhs = jnp.concatenate([wall[s, b, 0:GU, :] for s in (0, 1)], axis=0)
            dx = dot(dgu[2 * g + n], rhs, TN).astype(BF16)
            own = j % 16 - 2 * b
            spread_last = pick((i_ == MOST * (j // 16) + 16 + own) & (own >= 0) & (own < 2))
            out = dot(spread, dx).astype(BF16)
            last = last + dot(spread_last, dx)
            for k in range(EXPERTS):
                at = (k % 4) * MSG + b * 16
                dxp[g, 2 * n + k // 4, at:at + 16] = out[k * 16:k * 16 + 16]
        last = last.astype(BF16)
        for k in range(EXPERTS):
            at = (k % 4) * MSG + 128
            dxp[g, 2 * n + k // 4, at:at + 16] = last[k * 16:k * 16 + 16]
        dx_out(g, n).start()

    def dx_beside(g, dx):
        at = msg((x + dx) % NX)
        return remote(dxr.at[g, 1, at], dxn.at[g, at], dn_s.at[g, dx], dn_r.at[g, dx], beside)

    def sum_for_beside(g):
        dx_out(g, 1).wait_recv()
        for dx in (0, 1, 3, 2):
            at = msg((x + dx) % NX)
            dxr[g, 1, at] = (dxr[g, 1, at].astype(F32) + dxp[g, 2 + c, at].astype(F32)).astype(BF16)
            dx_beside(g, dx).start()

    backs = []
    back_own = pltpu.make_async_copy(dxr.at[0, 0, msg(x)], ret.at[msg(x * 2 + h)], loc)

    def send_back(g, dx):
        at = msg((x + dx) % NX)
        dx_beside(g, dx).wait_recv()
        total = dxr[g, 0, at].astype(F32) + dxp[g, c, at].astype(F32) + dxn[g, at].astype(F32)
        dxr[g, 0, at] = total.astype(BF16)
        if (dx, g) == (0, 0):
            back_own.start()
            return
        i = far.index((dx, g))
        backs.append(
            remote(
                dxr.at[g, 0, at], ret.at[msg(x * 2 + h)],
                ret_s.at[i], ret_r.at[i], {"dp": di, "expert": at_x(dx, g)},
            )
        )
        backs[-1].start()

    def rs(way, t, s):
        if t == 0:
            half = pl.ds(way * (WROWS // 2), WROWS // 2)
            src, dst = gr.at[s, (y + 4) % NY, half], rb.at[way, 0, s, half]
        else:
            src, dst = rb.at[way, t - 1, s], rb.at[way, t, s]
        return remote(
            src, dst, rs_s.at[way, t, s], rs_r.at[way, t, s], above if way == 0 else below
        )

    def weight_grads(s, b):
        cols = pl.ds(pl.multiple_of(b * BLK, BLK), BLK)
        gu, dn_ = jnp.zeros((GU, BLK), F32), jnp.zeros((HALF_HID, BLK), F32)
        for p in range(4):
            gu = gu + dot(dgu[p, s * GU:s * GU + GU], xs[part(p), cols])
            dn_ = dn_ + dot(hid[p, s * HALF_HID:s * HALF_HID + HALF_HID], ds[part(p), cols])
        gr[s, b, 0:GU, :] = gu.astype(BF16)
        gr[s, b, GU:WROWS, :] = dn_.astype(BF16)

    def grads_at(distance):
        for s in (1, 0):
            for b in sorted({distance, (NY - distance) % NY}):
                weight_grads(s, (y + b) % NY)

    def rs_add(way, t, s):
        rs(way, t, s).wait_recv()
        b = (y + 3 - t) % NY if way == 0 else (y - 3 + t + NY) % NY
        if t == 0:
            lo, hi = way * (WROWS // 2), (1 - way) * (WROWS // 2)
            a, o = pl.ds(lo, WROWS // 2), pl.ds(hi, WROWS // 2)
            rb[way, 0, s, a, :] = (rb[way, 0, s, a, :].astype(F32) + gr[s, b, a, :].astype(F32)).astype(BF16)
            rb[way, 0, s, o, :] = gr[s, b, o, :]
        else:
            rb[way, t, s] = (rb[way, t, s].astype(F32) + gr[s, b].astype(F32)).astype(BF16)

    def rs_step(t):
        for s in (1, 0):
            for way in (0, 1):
                rs_add(way, t, s)
                rs(way, t + 1, s).start()

    forward(7)
    wz.wait_recv()
    for way in (0, 1):
        ag(way, 0).start()
    for i in (1, 2, 3, 0):
        forward(i)
    ag_step(1)
    forward(4)
    ag_step(2)
    forward(5)
    ag_step(3)
    forward(6)
    for i in (7, 1, 2, 3):
        forward_beside(i)
    for k in range(1, NY):
        for w in own_block((y + k) % NY):
            w.wait()
    for n in (0, 1):
        gather_rows(0, n)
        activations(n, 0)
    for way in (0, 1):
        ag_in(way, 3)
    for n in (1, 0):
        activations(n, 1)
        input_grads(0, n)
    gather_rows(1, 0)
    activations(2, 0)
    activations(2, 1)
    for i in (0, 4, 5, 6):
        forward_beside(i)
    sum_for_beside(0)
    gather_rows(1, 1)
    for s in (1, 0):
        activations(3, s)
        weight_grads(s, (y + 4) % NY)
        for way in (0, 1):
            rs(way, 0, s).start()
    input_grads(1, 1)
    sum_for_beside(1)
    input_grads(1, 0)
    grads_at(3)
    dx_out(0, 0).wait_recv()
    rs_step(0)
    for dx in (0, 1, 3, 2):
        send_back(0, dx)
    dx_out(1, 0).wait_recv()
    for dx in (0, 1):
        send_back(1, dx)
    grads_at(2)
    for dx in (3, 2):
        send_back(1, dx)
    rs_step(1)
    grads_at(1)
    rs_step(2)
    grads_at(0)

    for w in [wz] + sends:
        w.wait_send()
    for g in (0, 1):
        for dx in range(NX):
            dx_beside(g, dx).wait_send()
        for n in (0, 1):
            dx_out(g, n).wait_send()
    for i in range(8):
        to_beside(i).wait_send()
        for n in (0, 1):
            to_sibling(n, i).wait_send()
    for way in (0, 1):
        for t in range(4):
            ag(way, t).wait_send()
        for t in range(3):
            for s in (0, 1):
                rs(way, t, s).wait_send()

    finals = []
    for s in (1, 0):
        for way in (0, 1):
            rs(way, 3, s).wait_recv()
        total = gr[s, y].astype(F32) + rb[0, 3, s].astype(F32) + rb[1, 3, s].astype(F32)
        for core in (0, 1):
            tot[s, core] = total[:, core * 128:core * 128 + 128].astype(BF16)
        if s:
            for core in (0, 1):
                finals.append(
                    remote(tot.at[1, core], zb.at[1, c], zs_s.at[core], zs_r.at[1, c], mirror(core))
                )
                finals[-1].start()
        else:
            finals.append(remote(tot.at[0, 1 - c], zb.at[0, c], zs_s.at[2], zs_r.at[0, c], sibling))
            finals[-1].start()
            zb[0, c] = tot[0, c]

    back_own.wait()
    for b in backs:
        b.wait_recv()

    def column(row):
        held = jnp.sum(jnp.where(diagonal, row.astype(F32), 0.0), axis=1, keepdims=True)
        return held.astype(jnp.int32)

    route, rank = column(route), column(rank)
    cols_of = iota((TOK, EXPERTS * 32), 1)
    for b in range(NY):
        at = jnp.where(rank < 16, route * 16 + rank, 112 + route * 16 + 2 * b + rank)
        take = pick(cols_of == at)
        rows = packed([(ret, (), k * MSG) for k in range(EXPERTS)], b * 16, 16)
        gin[:, b * BLK:b * BLK + BLK] = dot(take, rows).astype(BF16)
    store = pltpu.make_async_copy(gin, gin_out, io_s.at[2])
    store.start()

    remote(tot.at[0, c], zb.at[0, 1 - c], zs_s.at[0], zs_r.at[0, 1 - c], sibling).wait_recv()
    for core in (0, 1):
        remote(tot.at[1, core], zb.at[1, core], zs_s.at[0], zs_r.at[1, core], sibling).wait_recv()
    for core in (0, 1):
        acc = zb[0, core].astype(F32) + zb[1, core].astype(F32)
        for m in range(3):
            grads[m, core * HALF_HID:(core + 1) * HALF_HID] = acc[m * HALF_HID:(m + 1) * HALF_HID]

    store.wait()
    for w in finals + backs:
        w.wait_send()
    for way in (0, 1):
        for s in (0, 1):
            rs(way, 3, s).wait_send()


def body(tokens, cotangent, routes, expert_gates, gate_proj, up_proj, down_proj):
    vmem = pl.BlockSpec(memory_space=pltpu.VMEM)
    dma = pltpu.SemaphoreType.DMA
    anywhere = pl.BlockSpec(memory_space=pl.ANY)
    gin, grads = pl.pallas_call(
        kernel,
        out_shape=(
            jax.ShapeDtypeStruct((TOK, D), BF16),
            jax.ShapeDtypeStruct((3, GU, 128), F32),
        ),
        in_specs=[vmem] * 2 + [anywhere] * 5,
        out_specs=(anywhere, vmem),
        scratch_shapes=[
            pltpu.VMEM((EXPERTS * MSG, WIDE), BF16),
            pltpu.VMEM((2, NY, WROWS, BLK), BF16),
            pltpu.VMEM((4, EXPERTS * MSG, WIDE), BF16),
            pltpu.VMEM((4 * ROWS, D), BF16),
            pltpu.VMEM((4 * ROWS, D), BF16),
            pltpu.VMEM((2, NY, WROWS, BLK), BF16),
            pltpu.VMEM((2, 4, 2, WROWS, BLK), BF16),
            pltpu.VMEM((2, 2, WROWS, 128), BF16),
            pltpu.VMEM((2, 2, WROWS, 128), BF16),
            pltpu.VMEM((2, 4, NX * MSG, BLK), BF16),
            pltpu.VMEM((2, 2, NX * MSG, BLK), BF16),
            pltpu.VMEM((2, NX * MSG, BLK), BF16),
            pltpu.VMEM((EXPERTS * MSG, BLK), BF16),
            pltpu.VMEM((4, 2 * GU, ROWS), BF16),
            pltpu.VMEM((4, 2 * HALF_HID, ROWS), BF16),
            pltpu.VMEM((TOK, D), BF16),
            pltpu.VMEM((TOK, D), BF16),
            pltpu.VMEM((TOK, D), BF16),
            dma((3,)),
            dma((NY, 3)), dma((7,)), dma((7,)), dma, dma((8,)), dma((8,)), dma((2, 8)), dma((2, 8)),
            dma, dma, dma((2, 4)), dma((2, 4)), dma((2, 2)), dma((2, 2)), dma((2, NX)), dma((2, NX)),
            dma((7,)), dma((7,)), dma((2, 4, 2)), dma((2, 4, 2)), dma((3,)), dma((2, 2)),
        ],
        compiler_params=pltpu.CompilerParams(
            collective_id=0, has_side_effects=True, vmem_limit_bytes=56 * 2**20
        ),
    )(
        routes.reshape(1, TOK), expert_gates.reshape(1, TOK), tokens, cotangent,
        gate_proj.T, up_proj.T, down_proj,
    )
    return gin, grads[0].T, grads[1].T, grads[2]


def solution(mesh):
    in_specs = (
        P(("dp", "expert"), None),
        P(("dp", "expert"), None),
        P(("dp", "expert"), None),
        P(("dp", "expert"), None),
        P(None, "expert"),
        P(None, "expert"),
        P("expert", None),
    )
    out_specs = (P(("dp", "expert"), None), P("dp", "expert"), P("dp", "expert"), P("expert", "dp"))
    return jax.shard_map(body, mesh=mesh, in_specs=in_specs, out_specs=out_specs, check_vma=False)
```
